256 devices in a mesh: depth: 8 (over z), row: 4 (over y), col: 8 (over x, core).
Axes of the slice: x: 4, y: 4, z: 8, core: 2. Of those that a mesh axis runs over, the one named last changes fastest.
Arguments:
- a_tiles: bfloat16 [128, 40, 128, 128], P('row', 'depth', 'col'), may hold values from -6 to 6
- a_kcol: int32 [128, 40], P('row', 'depth'), may hold values from 0 to 15, as said below
- b_tiles: bfloat16 [128, 64, 128, 128], P('depth', 'col', 'row'), may hold values from -0.125 to 0.125
- b_jcol: int32 [128, 64], P('depth', 'col'), may hold values from 0 to 15, as said below
- c_jcol: int32 [128, 64], P('row', 'col'), may hold values from 0 to 15, as said below
- c_place: int32 [128, 64], P('row', 'col'), may hold values from 0 to 255, as said below
Outputs:
- c_owned: float32 [8192, 128, 128], P(('depth', 'row', 'col'))
The draws below stay inside these ranges and needn't reach their ends.
Inputs may be any that keep to these rules, and one draw needn't show every extreme that they name: Within one block row and one layer, the 5 entries a_kcol[i, d * 5 + s] are distinct. Within one block row and one column group, the 8 entries b_jcol[k, g * 8 + u] are distinct. Within one block row and one column group, the 8 entries c_jcol[i, g * 8 + v] are distinct. Over the kept blocks that share i // 32 and t // 8, c_place takes each value from 0 to 255 once.
All inputs are finite; a program needn't handle non-finite values.
Results may differ from the reference program's by a relative error of at most 0.0003.
Values may be sent and summed in bfloat16 or wider, within the bound.
No kernel may reach another device: no remote copies, remote signals or barrier semaphores. Data moves between devices by JAX's collectives and lax.ppermute only.
A program may use at most 128 MiB of HBM per device.

```python
import jax
import jax.numpy as jnp
from jax import lax

TILE = 128
ROWS_DEV = 32
K_DEV = 16
A_TILES = 5
B_TILES = 8
C_TILES = 8
COLS_GROUP = 16
NI = 128
NK = 128
KAT = 40
KBT = 64
KCT = 64
CAP = 4
OWNED = 32
NC = 8192
N_DEPTH = 8
N_ROW = 4
N_COL = 8


def pick_distinct(key, groups, pick_count, total):
    keys = jax.random.split(key, groups)
    return jax.vmap(lambda sub_key: jax.random.permutation(sub_key, total)[:pick_count])(keys)


def draw_a_kcol(key, part):
    key = jax.random.fold_in(key, 11)
    picks = pick_distinct(key, NI * N_DEPTH, A_TILES, K_DEV)
    return picks.reshape(NI, N_DEPTH * A_TILES).astype(jnp.int32)


def draw_b_jcol(key, part):
    key = jax.random.fold_in(key, 23)
    picks = pick_distinct(key, NK * N_COL, B_TILES, COLS_GROUP)
    return picks.reshape(NK, N_COL * B_TILES).astype(jnp.int32)


def draw_c_jcol(key, part):
    key = jax.random.fold_in(key, 37)
    picks = pick_distinct(key, NI * N_COL, C_TILES, COLS_GROUP)
    return picks.reshape(NI, N_COL * C_TILES).astype(jnp.int32)


def draw_c_place(key, part):
    key = jax.random.fold_in(key, 41)
    group_size = ROWS_DEV * C_TILES
    perms = pick_distinct(key, N_ROW * N_COL, group_size, group_size)
    perms = perms.reshape(N_ROW, N_COL, ROWS_DEV, C_TILES)
    perms = jnp.transpose(perms, (0, 2, 1, 3))
    return perms.reshape(NI, N_COL * C_TILES).astype(jnp.int32)


def block_scale(key, dims, pieces, smallest, top_value):
    def one(dim, parts):
        heights = jax.random.uniform(jax.random.fold_in(jax.random.fold_in(key, 6), dim), (parts,), jnp.float32, smallest / len(pieces), top_value / len(pieces))
        return jnp.repeat(jnp.exp(heights), dims[dim] // parts).reshape((-1,) + (1,) * (len(dims) - dim - 1))

    gain = one(*pieces[0])
    for cut in pieces[1:]:
        gain = gain * one(*cut)
    return gain


def bell_draw(own_key, shape, scale, bound, cuts=(), kind=jnp.bfloat16):
    gain = block_scale(own_key, shape, cuts, -0.22, 0.18) if cuts else 1.0
    entries = jax.random.normal(own_key, shape, jnp.float32) * scale * gain
    return jnp.minimum(jnp.maximum(entries, -bound), bound).astype(kind)


def setup_inputs(seed: int = 0) -> dict:
    key_of = jax.random.split(jax.random.key(seed), 7)
    return {
        "a_tiles": bell_draw(key_of[0], (NI, KAT, TILE, TILE), 1.0, 6.0, ((0, 4), (1, 8), (2, 8))),
        "a_kcol": draw_a_kcol(jax.random.fold_in(key_of[6], 71), 0),
        "b_tiles": bell_draw(key_of[2], (NK, KBT, TILE, TILE), (TILE * A_TILES * N_DEPTH // 2) ** -0.5, 0.125, ((0, 8), (1, 8), (2, 4))),
        "b_jcol": draw_b_jcol(jax.random.fold_in(key_of[6], 71), 0),
        "c_jcol": draw_c_jcol(jax.random.fold_in(key_of[6], 71), 0),
        "c_place": draw_c_place(jax.random.fold_in(key_of[6], 71), 0),
    }


def group_sums(a_tiles, a_kcol, b_tiles, b_jcol, c_jcol, row_id, group):
    layer_ids = jnp.arange(KAT, dtype=jnp.int32) // A_TILES
    a_row = a_tiles[row_id].astype(jnp.float32)
    k_global = (layer_ids * K_DEV + a_kcol[row_id]).astype(jnp.int32)
    col_ids = lax.dynamic_slice_in_dim(b_jcol[k_global], (group * B_TILES).astype(jnp.int32), B_TILES, 1)
    wanted = lax.dynamic_slice_in_dim(c_jcol[row_id], (group * C_TILES).astype(jnp.int32), C_TILES, 0)
    matches = col_ids[None, :, :] == wanted[:, None, None]
    slot_ids = jnp.arange(B_TILES, dtype=jnp.int32)
    chosen = jnp.sum(jnp.where(matches, slot_ids[None, None, :], 0), axis=2).astype(jnp.int32)
    located = jnp.any(matches, axis=2)
    picked = b_tiles[k_global[None, :], (group * B_TILES + chosen).astype(jnp.int32)].astype(jnp.float32)
    picked = jnp.where(located[:, :, None, None], picked, jnp.float32(0.0))
    return jnp.einsum("axy,tayz->txz", a_row, picked, precision=lax.Precision.HIGHEST)


def reference(a_tiles, a_kcol, b_tiles, b_jcol, c_jcol, c_place):
    def one_row(row_id):
        return lax.map(lambda group: group_sums(a_tiles, a_kcol, b_tiles, b_jcol, c_jcol, row_id, group),
                       jnp.arange(N_COL, dtype=jnp.int32))

    tile_sum = lax.map(one_row, jnp.arange(NI, dtype=jnp.int32)).reshape(NC, TILE, TILE)
    row_ids = jnp.arange(NI, dtype=jnp.int32)[:, None]
    tile_ids = jnp.arange(KCT, dtype=jnp.int32)[None, :]
    owner_id = c_place // CAP
    position = ((owner_id // N_COL * N_ROW + row_ids // ROWS_DEV) * N_COL + owner_id % N_COL) * OWNED
    position = (position + tile_ids // C_TILES * CAP + c_place % CAP).astype(jnp.int32)
    c_owned = jnp.zeros((NC, TILE, TILE), jnp.float32)
    return c_owned.at[position.reshape(NC)].set(tile_sum)
```

```python
import functools

import jax
import jax.numpy as jnp
from jax import lax
from jax.experimental import pallas as pl
from jax.experimental.pallas import tpu as pltpu
from jax.sharding import PartitionSpec as P

F32 = jnp.float32
I16 = jnp.int16
BF16 = jnp.bfloat16
VM = pltpu.VMEM
TOP = 32767.0
FINE = 128.0
TINY = 2.0**-110
TILE = 128
PART = 8
SUB = 16
ROWS = SUB * TILE
HALF_ROWS = PART * TILE
CODE_ROWS = 16


def select_blocks(a_kcol, b_jcol, c_jcol):
    k_rows, b_count = b_jcol.shape
    k_ids = jnp.arange(k_rows, dtype=jnp.int32)
    onehot_k = (a_kcol[:, :, None] == k_ids[None, None, :]).astype(jnp.int32)
    tile_cols = jnp.sum(onehot_k[:, :, :, None] * b_jcol[None, None, :, :], axis=2)
    matches = tile_cols[:, None, :, :] == c_jcol[:, :, None, None]
    slot_ids = jnp.arange(b_count, dtype=jnp.int32)
    chosen = jnp.sum(jnp.where(matches, slot_ids[None, None, None, :], 0), axis=3)
    located = jnp.any(matches, axis=3)
    flat_index = a_kcol[:, None, :] * b_count + chosen
    return jnp.where(located, flat_index, k_rows * b_count)


def make_table(a_kcol, b_jcol, c_jcol, c_place):
    picks = select_blocks(a_kcol, b_jcol, c_jcol)
    rows, kept, slots = picks.shape
    row_ids = jnp.broadcast_to(jnp.arange(rows, dtype=jnp.int32)[:, None, None], (rows, kept, 1))
    fields = jnp.concatenate([row_ids, picks], axis=2).reshape(rows * kept, slots + 1)
    q = jnp.arange(rows * kept, dtype=jnp.int32)
    target = q // 32 * 32 + q % 8 * 4 + q // 8 % 4
    hit = c_place.reshape(1, rows * kept) == target[:, None]
    table = jnp.sum(jnp.where(hit[:, :, None], fields[None], 0), axis=1)
    return table.reshape(rows * kept * (slots + 1))


def assemble_kernel(pos, a0, ap, al, ar, alp, arp, a2, a3, a2p, a3p, b0, bl, br, b2, b3, a_out, b_out, sem):
    row = pos[1]
    col = pos[2]
    other = col + 1 - 2 * (col % 2)
    half_a = a2.shape[0]
    half_b = b2.shape[0]
    count_a, count_b = a0.shape[0], b0.shape[0]

    def a_rows(c, lo, n):
        return a_out.at[pl.ds(lo, n), pl.ds(pl.multiple_of(c % 8 * 16, 16), 16), :]

    def b_rows(r, lo, n):
        return b_out.at[pl.ds(lo, n), pl.ds(pl.multiple_of(r % 4 * 32, 16), 32), :]

    copies = [
        (a0, a_rows(col, 0, count_a)),
        (ap, a_rows(other, 0, count_a)),
        (al, a_rows(col + 6, 0, count_a)),
        (ar, a_rows(col + 2, 0, count_a)),
        (alp, a_rows(other + 6, 0, count_a)),
        (arp, a_rows(other + 2, 0, count_a)),
        (a2, a_rows(col + 4, 0, half_a)),
        (a3, a_rows(col + 4, half_a, half_a)),
        (a2p, a_rows(other + 4, 0, half_a)),
        (a3p, a_rows(other + 4, half_a, half_a)),
        (b0, b_rows(row, 0, count_b)),
        (bl, b_rows(row + 3, 0, count_b)),
        (br, b_rows(row + 1, 0, count_b)),
        (b2, b_rows(row + 2, 0, half_b)),
        (b3, b_rows(row + 2, half_b, half_b)),
    ]
    started = [pltpu.make_async_copy(src, dst, sem.at[n]) for n, (src, dst) in enumerate(copies)]
    for one in started:
        one.start()
    b_out[count_b] = jnp.zeros(b_out.shape[1:], BF16)
    for one in started:
        one.wait()


def own_sum(tab, a, b, q):
    base = q * 6
    i = tab[base]
    left = jnp.concatenate([a[i * 5 + s] for s in range(5)], axis=1)
    right = jnp.concatenate([b[tab[base + 1 + s]] for s in range(5)], axis=0)
    return jnp.dot(left, right, preferred_element_type=F32)


def read_codes(ref, row, scale):
    codes = ref[pl.ds(row, CODE_ROWS), :].astype(jnp.int32).astype(F32)
    scale[...] = jnp.exp2(codes * (1.0 / FINE)) * (1.0 / TOP)


def decoded(ref, scale, t):
    rows = ref[pl.ds(pl.multiple_of(t * TILE, TILE), TILE), :]
    return rows.astype(jnp.int32).astype(F32) * scale[pl.ds(t, 1), :]


def encode(acc, out, row, codes, t):
    top = jnp.maximum(jnp.max(jnp.abs(acc), axis=0, keepdims=True), TINY)
    code = jnp.ceil(jnp.log2(top) * FINE) + 1.0
    codes[pl.ds(t, 1), :] = code
    quant = jnp.round(acc * (jnp.exp2(code * (-1.0 / FINE)) * TOP))
    out[pl.ds(row, TILE), :] = quant.astype(jnp.int32).astype(I16)


def write_codes(codes, out, row):
    out[pl.ds(row, CODE_ROWS), :] = codes[...].astype(jnp.int32).astype(I16)


def first_kernel(h, pos, tab, a, b, out_r, out_l, code_r, code_l):
    base = (pos[0] + 4) % 8 * 32 + h * SUB
    code_r[...] = jnp.zeros_like(code_r)
    code_l[...] = jnp.zeros_like(code_l)

    def body(g, carry):
        for u in range(2):
            t = g * 2 + u
            row = pl.multiple_of(t * TILE, TILE)
            encode(own_sum(tab, a, b, base + t), out_r, row, code_r, t)
            encode(own_sum(tab, a, b, base + PART + t), out_l, row, code_l, t)
        return carry

    lax.fori_loop(0, PART // 2, body, 0)
    write_codes(code_r, out_r, HALF_ROWS)
    write_codes(code_l, out_l, HALF_ROWS)


def second_kernel(h, pos, tab, a, b, in_r, in_l, out_r, out_l, code_r, code_l, scale_r, scale_l):
    base_r = (pos[0] + 3) % 8 * 32 + h * SUB
    base_l = (pos[0] + 5) % 8 * 32 + h * SUB
    read_codes(in_r, HALF_ROWS, scale_r)
    read_codes(in_l, HALF_ROWS, scale_l)

    def body(t, carry):
        row = pl.multiple_of(t * TILE, TILE)
        late = pl.multiple_of((t + PART) * TILE, TILE)
        encode(own_sum(tab, a, b, base_r + t) + decoded(in_r, scale_r, t), out_r, row, code_r, t)
        encode(own_sum(tab, a, b, base_r + PART + t), out_r, late, code_r, t + PART)
        encode(own_sum(tab, a, b, base_l + t), out_l, row, code_l, t)
        encode(own_sum(tab, a, b, base_l + PART + t) + decoded(in_l, scale_l, t), out_l, late, code_l, t + PART)
        return carry

    lax.fori_loop(0, PART, body, 0)
    write_codes(code_r, out_r, ROWS)
    write_codes(code_l, out_l, ROWS)


def middle_kernel(h, away, pos, tab, a, b, in_r, in_l, out_r, out_l, code_r, code_l, scale_r, scale_l):
    base_r = (pos[0] + away) % 8 * 32 + h * SUB
    base_l = (pos[0] + 8 - away) % 8 * 32 + h * SUB
    read_codes(in_r, ROWS, scale_r)
    read_codes(in_l, ROWS, scale_l)

    def body(g, carry):
        for u in range(2):
            t = g * 2 + u
            row = pl.multiple_of(t * TILE, TILE)
            encode(own_sum(tab, a, b, base_r + t) + decoded(in_r, scale_r, t), out_r, row, code_r, t)
            encode(own_sum(tab, a, b, base_l + t) + decoded(in_l, scale_l, t), out_l, row, code_l, t)
        return carry

    lax.fori_loop(0, SUB // 2, body, 0)
    write_codes(code_r, out_r, ROWS)
    write_codes(code_l, out_l, ROWS)


def last_kernel(h, pos, tab, a, b, in_r, in_l, out, code, scale_r, scale_l):
    base = pos[0] * 32 + h * SUB
    read_codes(in_r, ROWS, scale_r)
    read_codes(in_l, ROWS, scale_l)
    code[...] = jnp.zeros_like(code)

    def body(oc, carry):
        for ab in range(2):
            t = ab * PART + oc
            acc = own_sum(tab, a, b, base + t) + decoded(in_r, scale_r, t) + decoded(in_l, scale_l, t)
            encode(acc, out.at[oc], ab * TILE, code, ab)
        write_codes(code, out.at[oc], 2 * TILE)
        return carry

    lax.fori_loop(0, PART, body, 0)


def deliver_kernel(one, two, out, scale):
    def body(g, carry):
        for h, src in enumerate((one, two)):
            read_codes(src.at[g], 2 * TILE, scale)
            for ab in range(2):
                rows = src[g, pl.ds(ab * TILE, TILE), :].astype(jnp.int32).astype(F32)
                out[g * 4 + 2 * h + ab] = rows * scale[ab : ab + 1, :]
        return carry

    lax.fori_loop(0, out.shape[0] // 4, body, 0)


SMEM_SPEC = pl.BlockSpec(memory_space=pltpu.SMEM)
VMEM_SPEC = pl.BlockSpec(memory_space=pltpu.VMEM)
ANY_SPEC = pl.BlockSpec(memory_space=pl.ANY)


def params(mib):
    return pltpu.CompilerParams(vmem_limit_bytes=mib * 2**20)


def cost(tiles, bytes_accessed):
    return pl.CostEstimate(flops=tiles * 5 * 2 * TILE**3, bytes_accessed=bytes_accessed, transcendentals=0)


def scratch(count):
    return [pltpu.VMEM((CODE_ROWS, TILE), F32)] * count


def message(rows):
    return jax.ShapeDtypeStruct((rows + CODE_ROWS, TILE), I16)


def step(kernel, name, tiles, out_shape, scratches, *args):
    ins = [SMEM_SPEC, SMEM_SPEC] + [VMEM_SPEC] * (len(args) - 2)
    return pl.pallas_call(
        kernel,
        out_shape=out_shape,
        in_specs=ins,
        out_specs=jax.tree.map(lambda _: VMEM_SPEC, out_shape),
        scratch_shapes=scratch(scratches),
        compiler_params=params(16),
        cost_estimate=cost(tiles, 2**22),
        name=name,
    )(*args)


def deliver(one, two, tiles):
    return pl.pallas_call(
        deliver_kernel,
        out_shape=jax.ShapeDtypeStruct((tiles, TILE, TILE), F32),
        in_specs=[VMEM_SPEC] * 2,
        out_specs=VMEM_SPEC,
        scratch_shapes=scratch(1),
        compiler_params=params(16),
        cost_estimate=cost(0, 2**22),
        name="deliver",
    )(one, two)


def per_device(a_tiles, a_kcol, b_tiles, b_jcol, c_jcol, c_place):
    depth, row, col = (lax.axis_size(n) for n in ("depth", "row", "col"))

    def shift(axis, size, by):
        pairs = [(i, (i + by) % size) for i in range(size)]
        return lambda x: lax.ppermute(x, axis, pairs)

    y_up, y_down = shift("row", row, 1), shift("row", row, -1)
    x_up, x_down = shift("col", col, 2), shift("col", col, -2)
    z_up, z_down = shift("depth", depth, 1), shift("depth", depth, -1)

    def swap(x):
        return lax.ppermute(x, "col", [(i, i ^ 1) for i in range(col)])

    pos = jnp.stack([lax.axis_index(n) for n in ("depth", "row", "col")]).astype(jnp.int32)
    b0 = b_tiles.reshape((-1,) + b_tiles.shape[2:])
    a0 = a_tiles.reshape((-1,) + a_tiles.shape[2:])
    half_b, half_a = b0.shape[0] // 2, a0.shape[0] // 2
    bl, br = y_up(b0), y_down(b0)
    al, ar = x_up(a0), x_down(a0)
    ap = swap(a0)
    b2, b3 = y_up(bl[:half_b]), y_down(br[half_b:])
    a2, a3 = x_up(al[:half_a]), x_down(ar[half_a:])
    alp, arp, a2p, a3p = swap(al), swap(ar), swap(a2), swap(a3)
    tab = make_table(a_kcol, b_jcol, c_jcol, c_place)
    a, b = pl.pallas_call(
        assemble_kernel,
        out_shape=(VM((a0.shape[0], TILE, TILE), BF16), VM((b0.shape[0] + 1, TILE, TILE), BF16)),
        in_specs=[SMEM_SPEC] + [ANY_SPEC] * 15,
        out_specs=(VMEM_SPEC, VMEM_SPEC),
        scratch_shapes=[pltpu.SemaphoreType.DMA((15,))],
        compiler_params=params(16),
        cost_estimate=cost(0, 9 * 2**20),
        name="assemble",
    )(pos, a0, ap, al, ar, alp, arp, a2, a3, a2p, a3p, b0, bl, br, b2, b3)

    short = (message(HALF_ROWS),) * 2
    full = (message(ROWS),) * 2
    flying = []
    for h in range(2):
        r, l = step(functools.partial(first_kernel, h), f"first{h}", 16, short, 2, pos, tab, a, b)
        flying.append((z_up(r), z_down(l)))
    for hop in range(3):
        landed, flying = flying, []
        for h in range(2):
            if hop == 0:
                kernel, name = functools.partial(second_kernel, h), f"second{h}"
            else:
                kernel, name = functools.partial(middle_kernel, h, 3 - hop), f"middle{hop}{h}"
            r, l = step(kernel, name, 32, full, 4, pos, tab, a, b, *landed[h])
            flying.append((z_up(r), z_down(l)))
    arrived = []
    for h in range(2):
        out = jax.ShapeDtypeStruct((col, 2 * TILE + CODE_ROWS, TILE), I16)
        mine = step(functools.partial(last_kernel, h), f"last{h}", 16, out, 3, pos, tab, a, b, *flying[h])
        arrived.append(lax.all_to_all(mine, "col", split_axis=0, concat_axis=0, tiled=True))
    return deliver(*arrived, col * 4)


def solution(mesh):
    return jax.shard_map(
        per_device,
        mesh=mesh,
        in_specs=(
            P("row", "depth", "col", None),
            P("row", "depth"),
            P("depth", "col", "row", None),
            P("depth", "col"),
            P("row", "col"),
            P("row", "col"),
        ),
        out_specs=P(("depth", "row", "col"), None, None),
        check_vma=False,
    )
```

```python
import functools

import jax
import jax.numpy as jnp
from jax import lax
from jax.experimental import pallas as pl
from jax.experimental.pallas import tpu as pltpu
from jax.sharding import PartitionSpec as P

F32 = jnp.float32
I16 = jnp.int16
BF16 = jnp.bfloat16
VM = pltpu.VMEM
TOP = 32767.0
FINE = 128.0
TINY = 2.0**-110
TILE = 128
PART = 8
SUB = 16
ROWS = SUB * TILE
HALF_ROWS = PART * TILE
CODE_ROWS = 16


def select_blocks(a_kcol, b_jcol, c_jcol):
    k_rows, b_count = b_jcol.shape
    k_ids = jnp.arange(k_rows, dtype=jnp.int32)
    onehot_k = (a_kcol[:, :, None] == k_ids[None, None, :]).astype(jnp.int32)
    tile_cols = jnp.sum(onehot_k[:, :, :, None] * b_jcol[None, None, :, :], axis=2)
    matches = tile_cols[:, None, :, :] == c_jcol[:, :, None, None]
    slot_ids = jnp.arange(b_count, dtype=jnp.int32)
    chosen = jnp.sum(jnp.where(matches, slot_ids[None, None, None, :], 0), axis=3)
    located = jnp.any(matches, axis=3)
    flat_index = a_kcol[:, None, :] * b_count + chosen
    return jnp.where(located, flat_index, k_rows * b_count)


def make_table(a_kcol, b_jcol, c_jcol, c_place):
    picks = select_blocks(a_kcol, b_jcol, c_jcol)
    rows, kept, slots = picks.shape
    row_ids = jnp.broadcast_to(jnp.arange(rows, dtype=jnp.int32)[:, None, None], (rows, kept, 1))
    fields = jnp.concatenate([row_ids, picks], axis=2).reshape(rows * kept, slots + 1)
    q = jnp.arange(rows * kept, dtype=jnp.int32)
    target = q // 32 * 32 + q % 8 * 4 + q // 8 % 4
    hit = c_place.reshape(1, rows * kept) == target[:, None]
    table = jnp.sum(jnp.where(hit[:, :, None], fields[None], 0), axis=1)
    return table.reshape(rows * kept * (slots + 1))


def a_place(a_out, col):
    return a_out.at[:, pl.ds(pl.multiple_of((col + 8) % 8 * 16, 16), 16), :]


def b_place(b_out, row, count):
    return b_out.at[pl.ds(0, count), pl.ds(pl.multiple_of(row % 4 * 32, 32), 32), :]


def copy_all(copies, sem):
    started = [pltpu.make_async_copy(src, dst, sem.at[n]) for n, (src, dst) in enumerate(copies)]
    for one in started:
        one.start()
    return started


def assemble_kernel(pos, a0, ap, p1, p2, p3, s1, s2, s3, b0, q1, t2, a_out, b_out, sem):
    row, col = pos[1], pos[2]
    core = col % 2
    other = col + 1 - 2 * core
    ahead = 4 * core - 2
    count = b0.shape[0]
    copies = [
        (a0, a_place(a_out, col)),
        (ap, a_place(a_out, other)),
        (p1, a_place(a_out, col + ahead)),
        (p2, a_place(a_out, other + ahead)),
        (p3, a_place(a_out, col + 4)),
        (s1, a_place(a_out, other - ahead)),
        (s2, a_place(a_out, col - ahead)),
        (s3, a_place(a_out, other + 4)),
        (b0, b_place(b_out, row, count)),
        (q1, b_place(b_out, row + 3 + 2 * core, count)),
        (t2, b_place(b_out, row + 1 + 2 * core, count)),
    ]
    started = copy_all(copies, sem)
    b_out[count] = jnp.zeros(b_out.shape[1:], BF16)
    for one in started:
        one.wait()


def own_sum(tab, a, b, q):
    base = q * 6
    i = tab[base]
    left = jnp.concatenate([a[i * 5 + s] for s in range(5)], axis=1)
    right = jnp.concatenate([b[tab[base + 1 + s]] for s in range(5)], axis=0)
    return jnp.dot(left, right, preferred_element_type=F32)


def read_codes(ref, row, scale):
    codes = ref[pl.ds(row, CODE_ROWS), :].astype(jnp.int32).astype(F32)
    scale[...] = jnp.exp2(codes * (1.0 / FINE)) * (1.0 / TOP)


def decoded(ref, scale, t):
    rows = ref[pl.ds(pl.multiple_of(t * TILE, TILE), TILE), :]
    return rows.astype(jnp.int32).astype(F32) * scale[pl.ds(t, 1), :]


def encode(acc, out, row, codes, t):
    top = jnp.maximum(jnp.max(jnp.abs(acc), axis=0, keepdims=True), TINY)
    code = jnp.ceil(jnp.log2(top) * FINE) + 1.0
    codes[pl.ds(t, 1), :] = code
    quant = jnp.round(acc * (jnp.exp2(code * (-1.0 / FINE)) * TOP))
    out[pl.ds(row, TILE), :] = quant.astype(jnp.int32).astype(I16)


def write_codes(codes, out, row):
    out[pl.ds(row, CODE_ROWS), :] = codes[...].astype(jnp.int32).astype(I16)


def finish_kernel(pos, tab, a, b_in, q3, out_r, out_l, b, code_r, code_l, sem):
    late = pltpu.make_async_copy(q3, b_place(b, pos[1] + 2, q3.shape[0]), sem)
    late.start()
    late.wait()
    first_kernel(0, pos, tab, a, b, out_r, out_l, code_r, code_l)


def first_kernel(h, pos, tab, a, b, out_r, out_l, code_r, code_l):
    base = (pos[0] + 4) % 8 * 32 + h * SUB
    code_r[...] = jnp.zeros_like(code_r)
    code_l[...] = jnp.zeros_like(code_l)

    def body(g, carry):
        for u in range(2):
            t = g * 2 + u
            row = pl.multiple_of(t * TILE, TILE)
            encode(own_sum(tab, a, b, base + t), out_r, row, code_r, t)
            encode(own_sum(tab, a, b, base + PART + t), out_l, row, code_l, t)
        return carry

    lax.fori_loop(0, PART // 2, body, 0)
    write_codes(code_r, out_r, HALF_ROWS)
    write_codes(code_l, out_l, HALF_ROWS)


def second_kernel(h, pos, tab, a, b, in_r, in_l, out_r, out_l, code_r, code_l, scale_r, scale_l):
    base_r = (pos[0] + 3) % 8 * 32 + h * SUB
    base_l = (pos[0] + 5) % 8 * 32 + h * SUB
    read_codes(in_r, HALF_ROWS, scale_r)
    read_codes(in_l, HALF_ROWS, scale_l)

    def body(t, carry):
        row = pl.multiple_of(t * TILE, TILE)
        late = pl.multiple_of((t + PART) * TILE, TILE)
        encode(own_sum(tab, a, b, base_r + t) + decoded(in_r, scale_r, t), out_r, row, code_r, t)
        encode(own_sum(tab, a, b, base_r + PART + t), out_r, late, code_r, t + PART)
        encode(own_sum(tab, a, b, base_l + t), out_l, row, code_l, t)
        encode(own_sum(tab, a, b, base_l + PART + t) + decoded(in_l, scale_l, t), out_l, late, code_l, t + PART)
        return carry

    lax.fori_loop(0, PART, body, 0)
    write_codes(code_r, out_r, ROWS)
    write_codes(code_l, out_l, ROWS)


def middle_kernel(h, away, pos, tab, a, b, in_r, in_l, out_r, out_l, code_r, code_l, scale_r, scale_l):
    base_r = (pos[0] + away) % 8 * 32 + h * SUB
    base_l = (pos[0] + 8 - away) % 8 * 32 + h * SUB
    read_codes(in_r, ROWS, scale_r)
    read_codes(in_l, ROWS, scale_l)

    def body(g, carry):
        for u in range(2):
            t = g * 2 + u
            row = pl.multiple_of(t * TILE, TILE)
            encode(own_sum(tab, a, b, base_r + t) + decoded(in_r, scale_r, t), out_r, row, code_r, t)
            encode(own_sum(tab, a, b, base_l + t) + decoded(in_l, scale_l, t), out_l, row, code_l, t)
        return carry

    lax.fori_loop(0, SUB // 2, body, 0)
    write_codes(code_r, out_r, ROWS)
    write_codes(code_l, out_l, ROWS)


def own_kernel(pos, tab, a, b, own):
    def body(g, carry):
        for u in range(4):
            own[g * 4 + u] = own_sum(tab, a, b, pos[0] * 32 + g * 4 + u)
        return carry

    lax.fori_loop(0, own.shape[0] // 4, body, 0)


def last_kernel(h, own, in_r, in_l, out, code, scale_r, scale_l):
    read_codes(in_r, ROWS, scale_r)
    read_codes(in_l, ROWS, scale_l)
    code[...] = jnp.zeros_like(code)

    def body(g, carry):
        for u in range(2):
            oc = g * 2 + u
            for ab in range(2):
                t = ab * PART + oc
                acc = own[h * SUB + t] + decoded(in_r, scale_r, t) + decoded(in_l, scale_l, t)
                encode(acc, out.at[oc], ab * TILE, code.at[u], ab)
            write_codes(code.at[u], out.at[oc], 2 * TILE)
        return carry

    lax.fori_loop(0, PART // 2, body, 0)


def deliver_kernel(one, two, out, scale):
    def body(g, carry):
        for h, src in enumerate((one, two)):
            read_codes(src.at[g], 2 * TILE, scale)
            for ab in range(2):
                rows = src[g, pl.ds(ab * TILE, TILE), :].astype(jnp.int32).astype(F32)
                out[g * 4 + 2 * h + ab] = rows * scale[ab : ab + 1, :]
        return carry

    lax.fori_loop(0, out.shape[0] // 4, body, 0)


SMEM_SPEC = pl.BlockSpec(memory_space=pltpu.SMEM)
VMEM_SPEC = pl.BlockSpec(memory_space=pltpu.VMEM)
ANY_SPEC = pl.BlockSpec(memory_space=pl.ANY)


def params(mib):
    return pltpu.CompilerParams(vmem_limit_bytes=mib * 2**20)


COST_FIRST = 2
COST_SECOND0 = 3
COST_SECOND1 = 3
COST_MIDDLE = 3
COST_OWN = 3
COST_LAST = 1


def cost(us):
    return pl.CostEstimate(flops=int(us * 1e9), bytes_accessed=int(us * 3e6), transcendentals=0)


def scratch(count):
    return [pltpu.VMEM((CODE_ROWS, TILE), F32)] * count


def message(rows):
    return jax.ShapeDtypeStruct((rows + CODE_ROWS, TILE), I16)


def step(kernel, name, weight, out_shape, scratches, after, *args):
    ins = [SMEM_SPEC, SMEM_SPEC] + [VMEM_SPEC] * (len(args) - 2) + [ANY_SPEC]
    count = len(args)

    def body(*refs):
        kernel(*refs[:count], *refs[count + 1 :])

    return pl.pallas_call(
        body,
        out_shape=out_shape,
        in_specs=ins,
        out_specs=jax.tree.map(lambda _: VMEM_SPEC, out_shape),
        scratch_shapes=scratch(scratches),
        compiler_params=params(16),
        cost_estimate=cost(weight),
        name=name,
    )(*args, after)


def own_tiles(after, *args):
    def body(pos, tab, a, b, unused, own):
        own_kernel(pos, tab, a, b, own)

    return pl.pallas_call(
        body,
        out_shape=VM((2 * SUB, TILE, TILE), F32),
        in_specs=[SMEM_SPEC] * 2 + [VMEM_SPEC] * 2 + [ANY_SPEC],
        out_specs=VMEM_SPEC,
        compiler_params=params(16),
        cost_estimate=cost(COST_OWN),
        name="own",
    )(*args, after)


def last(h, out_shape, after, *args):
    def body(own, in_r, in_l, unused, *rest):
        last_kernel(h, own, in_r, in_l, *rest)

    return pl.pallas_call(
        body,
        out_shape=out_shape,
        in_specs=[VMEM_SPEC] * 3 + [ANY_SPEC],
        out_specs=VMEM_SPEC,
        scratch_shapes=[pltpu.VMEM((2, CODE_ROWS, TILE), F32)] + scratch(2),
        compiler_params=params(16),
        cost_estimate=cost(COST_LAST),
        name=f"last{h}",
    )(*args, after)


def deliver(one, two, tiles):
    return pl.pallas_call(
        deliver_kernel,
        out_shape=jax.ShapeDtypeStruct((tiles, TILE, TILE), F32),
        in_specs=[VMEM_SPEC] * 2,
        out_specs=VMEM_SPEC,
        scratch_shapes=scratch(1),
        compiler_params=params(16),
        cost_estimate=cost(0),
        name="deliver",
    )(one, two)


def per_device(a_tiles, a_kcol, b_tiles, b_jcol, c_jcol, c_place):
    depth, row, col = (lax.axis_size(n) for n in ("depth", "row", "col"))

    def shift(axis, size, by):
        pairs = [(i, (i + by) % size) for i in range(size)]
        return lambda x: lax.ppermute(x, axis, pairs)

    def x_split(x):
        return lax.ppermute(x, "col", [(i, (i + 2 - 4 * (i % 2)) % col) for i in range(col)])

    def y_split(x):
        pairs = []
        for r in range(row):
            for c in range(col):
                pairs.append((r * col + c, (r + 1 - 2 * (c % 2)) % row * col + c))
        return lax.ppermute(x, ("row", "col"), pairs)

    z_up, z_down = shift("depth", depth, 1), shift("depth", depth, -1)

    def swap(x):
        return lax.ppermute(x, "col", [(i, i ^ 1) for i in range(col)])

    pos = jnp.stack([lax.axis_index(n) for n in ("depth", "row", "col")]).astype(jnp.int32)
    b0 = b_tiles.reshape((-1,) + b_tiles.shape[2:])
    a0 = a_tiles.reshape((-1,) + a_tiles.shape[2:])
    q1, p1 = y_split(b0), x_split(a0)
    bp, ap = swap(b0), swap(a0)
    q2, p2 = y_split(bp), x_split(ap)
    q3, p3 = y_split(q1), x_split(p1)
    t2, s1, s2, s3 = swap(q2), swap(p1), swap(p2), swap(p3)
    tab = make_table(a_kcol, b_jcol, c_jcol, c_place)
    b_vmem = VM((b0.shape[0] + 1, TILE, TILE), BF16)
    a, b = pl.pallas_call(
        assemble_kernel,
        out_shape=(VM((a0.shape[0], TILE, TILE), BF16), b_vmem),
        in_specs=[SMEM_SPEC] + [ANY_SPEC] * 11,
        out_specs=(VMEM_SPEC, VMEM_SPEC),
        scratch_shapes=[pltpu.SemaphoreType.DMA((11,))],
        compiler_params=params(16),
        cost_estimate=cost(0),
        name="assemble",
    )(pos, a0, ap, p1, p2, p3, s1, s2, s3, b0, q1, t2)

    short = (message(HALF_ROWS),) * 2
    full = (message(ROWS),) * 2
    flying = []
    for h in range(2):
        if h == 0:
            r, l, b = pl.pallas_call(
                finish_kernel,
                out_shape=short + (b_vmem,),
                in_specs=[SMEM_SPEC] * 2 + [VMEM_SPEC] * 2 + [ANY_SPEC],
                out_specs=(VMEM_SPEC,) * 3,
                scratch_shapes=scratch(2) + [pltpu.SemaphoreType.DMA],
                input_output_aliases={3: 2},
                compiler_params=params(16),
                cost_estimate=cost(COST_FIRST),
                name="first0",
            )(pos, tab, a, b, q3)
        else:
            r, l = step(functools.partial(first_kernel, h), f"first{h}", COST_FIRST, short, 2, r, pos, tab, a, b)
        flying.append((z_up(r), z_down(l)))
    for hop in range(3):
        landed, flying = flying, []
        for h in range(2):
            if hop == 0:
                kernel, name = functools.partial(second_kernel, h), f"second{h}"
            else:
                kernel, name = functools.partial(middle_kernel, h, 3 - hop), f"middle{hop}{h}"
            weight = (COST_SECOND0, COST_SECOND1)[h] if hop == 0 else COST_MIDDLE
            r, l = step(kernel, name, weight, full, 4, r, pos, tab, a, b, *landed[h])
            flying.append((z_up(r), z_down(l)))
    own = own_tiles(r, pos, tab, a, b)
    arrived = []
    for h in range(2):
        out = jax.ShapeDtypeStruct((col, 2 * TILE + CODE_ROWS, TILE), I16)
        r = last(h, out, r, own, *flying[h])
        if arrived:
            r, arrived[0] = lax.optimization_barrier((r, arrived[0]))
        arrived.append(lax.all_to_all(r, "col", split_axis=0, concat_axis=0, tiled=True))
    return deliver(*arrived, col * 4)


def solution(mesh):
    return jax.shard_map(
        per_device,
        mesh=mesh,
        in_specs=(
            P("row", "depth", "col", None),
            P("row", "depth"),
            P("depth", "col", "row", None),
            P("depth", "col"),
            P("row", "col"),
            P("row", "col"),
        ),
        out_specs=P(("depth", "row", "col"), None, None),
        check_vma=False,
    )
```

```python
import functools

import jax
import jax.numpy as jnp
from jax import lax
from jax.experimental import pallas as pl
from jax.experimental.pallas import tpu as pltpu
from jax.sharding import PartitionSpec as P

F32 = jnp.float32
I16 = jnp.int16
BF16 = jnp.bfloat16
VM = pltpu.VMEM
TOP = 32767.0
FINE = 128.0
TINY = 2.0**-110
TILE = 128
PART = 8
SUB = 16
ROWS = SUB * TILE
HALF_ROWS = PART * TILE
CODE_ROWS = 16


def select_blocks(a_kcol, b_jcol, c_jcol):
    k_rows, b_count = b_jcol.shape
    k_ids = jnp.arange(k_rows, dtype=jnp.int32)
    onehot_k = (a_kcol[:, :, None] == k_ids[None, None, :]).astype(jnp.int32)
    tile_cols = jnp.sum(onehot_k[:, :, :, None] * b_jcol[None, None, :, :], axis=2)
    matches = tile_cols[:, None, :, :] == c_jcol[:, :, None, None]
    slot_ids = jnp.arange(b_count, dtype=jnp.int32)
    chosen = jnp.sum(jnp.where(matches, slot_ids[None, None, None, :], 0), axis=3)
    located = jnp.any(matches, axis=3)
    flat_index = a_kcol[:, None, :] * b_count + chosen
    return jnp.where(located, flat_index, k_rows * b_count)


ORDER = (
    [(2, k, j) for k in range(2) for j in range(4)]
    + [(d, k, j) for d in (1, 3) for k in range(2) for j in (0, 1)]
    + [(d, k, j) for d in (1, 3) for k in range(2) for j in (2, 3)]
    + [(0, k, j) for k in range(2) for j in range(4)]
)


def make_table(a_kcol, b_jcol, c_jcol, c_place):
    col = lax.axis_index("col")
    away, core, tile = (jnp.array([entry[n] for entry in ORDER], jnp.int32) for n in range(3))
    owner = (col // 2 + away) % 4 * 2 + (col + core) % 2
    picks = select_blocks(a_kcol, b_jcol, c_jcol)
    rows, kept, slots = picks.shape
    row_ids = jnp.broadcast_to(jnp.arange(rows, dtype=jnp.int32)[:, None, None], (rows, kept, 1))
    fields = jnp.concatenate([row_ids, picks], axis=2).reshape(rows * kept, slots + 1)
    q = jnp.arange(rows * kept, dtype=jnp.int32)
    target = q // 32 * 32 + jnp.tile(owner * 4 + tile, rows * kept // 32)
    hit = c_place.reshape(1, rows * kept) == target[:, None]
    table = jnp.sum(jnp.where(hit[:, :, None], fields[None], 0), axis=1)
    return table.reshape(rows * kept * (slots + 1))


def a_place(a_out, col):
    return a_out.at[:, pl.ds(pl.multiple_of((col + 8) % 8 * 16, 16), 16), :]


def b_place(b_out, row, count):
    return b_out.at[pl.ds(0, count), pl.ds(pl.multiple_of(row % 4 * 32, 32), 32), :]


def copy_all(copies, sem):
    started = [pltpu.make_async_copy(src, dst, sem.at[n]) for n, (src, dst) in enumerate(copies)]
    for one in started:
        one.start()
    return started


def assemble_kernel(pos, a0, ap, p1, p2, p3, s1, s2, s3, b0, q1, t2, a_out, b_out, sem):
    row, col = pos[1], pos[2]
    core = col % 2
    other = col + 1 - 2 * core
    ahead = 4 * core - 2
    count = b0.shape[0]
    copies = [
        (a0, a_place(a_out, col)),
        (ap, a_place(a_out, other)),
        (p1, a_place(a_out, col + ahead)),
        (p2, a_place(a_out, other + ahead)),
        (p3, a_place(a_out, col + 4)),
        (s1, a_place(a_out, other - ahead)),
        (s2, a_place(a_out, col - ahead)),
        (s3, a_place(a_out, other + 4)),
        (b0, b_place(b_out, row, count)),
        (q1, b_place(b_out, row + 3 + 2 * core, count)),
        (t2, b_place(b_out, row + 1 + 2 * core, count)),
    ]
    started = copy_all(copies, sem)
    b_out[count] = jnp.zeros(b_out.shape[1:], BF16)
    for one in started:
        one.wait()


def own_sum(tab, a, b, q):
    base = q * 6
    i = tab[base]
    left = jnp.concatenate([a[i * 5 + s] for s in range(5)], axis=1)
    right = jnp.concatenate([b[tab[base + 1 + s]] for s in range(5)], axis=0)
    return jnp.dot(left, right, preferred_element_type=F32)


def read_codes(ref, row, scale):
    codes = ref[pl.ds(row, CODE_ROWS), :].astype(jnp.int32).astype(F32)
    scale[...] = jnp.exp2(codes * (1.0 / FINE)) * (1.0 / TOP)


def decoded(ref, scale, t):
    rows = ref[pl.ds(pl.multiple_of(t * TILE, TILE), TILE), :]
    return rows.astype(jnp.int32).astype(F32) * scale[pl.ds(t, 1), :]


def encode(acc, out, row, codes, t):
    top = jnp.maximum(jnp.max(jnp.abs(acc), axis=0, keepdims=True), TINY)
    code = jnp.ceil(jnp.log2(top) * FINE) + 1.0
    codes[pl.ds(t, 1), :] = code
    quant = jnp.round(acc * (jnp.exp2(code * (-1.0 / FINE)) * TOP))
    out[pl.ds(row, TILE), :] = quant.astype(jnp.int32).astype(I16)


def write_codes(codes, out, row):
    out[pl.ds(row, CODE_ROWS), :] = codes[...].astype(jnp.int32).astype(I16)


def finish_kernel(pos, tab, a, b_in, q3, out_r, out_l, b, code_r, code_l, sem):
    late = pltpu.make_async_copy(q3, b_place(b, pos[1] + 2, q3.shape[0]), sem)
    late.start()
    late.wait()
    first_kernel(0, pos, tab, a, b, out_r, out_l, code_r, code_l)


def first_kernel(h, pos, tab, a, b, out_r, out_l, code_r, code_l):
    base = (pos[0] + 4) % 8 * 32 + h * SUB
    code_r[...] = jnp.zeros_like(code_r)
    code_l[...] = jnp.zeros_like(code_l)

    def body(g, carry):
        for u in range(2):
            t = g * 2 + u
            row = pl.multiple_of(t * TILE, TILE)
            encode(own_sum(tab, a, b, base + t), out_r, row, code_r, t)
            encode(own_sum(tab, a, b, base + PART + t), out_l, row, code_l, t)
        return carry

    lax.fori_loop(0, PART // 2, body, 0)
    write_codes(code_r, out_r, HALF_ROWS)
    write_codes(code_l, out_l, HALF_ROWS)


def second_kernel(h, pos, tab, a, b, in_r, in_l, out_r, out_l, code_r, code_l, scale_r, scale_l):
    base_r = (pos[0] + 3) % 8 * 32 + h * SUB
    base_l = (pos[0] + 5) % 8 * 32 + h * SUB
    read_codes(in_r, HALF_ROWS, scale_r)
    read_codes(in_l, HALF_ROWS, scale_l)

    def body(t, carry):
        row = pl.multiple_of(t * TILE, TILE)
        late = pl.multiple_of((t + PART) * TILE, TILE)
        encode(own_sum(tab, a, b, base_r + t) + decoded(in_r, scale_r, t), out_r, row, code_r, t)
        encode(own_sum(tab, a, b, base_r + PART + t), out_r, late, code_r, t + PART)
        encode(own_sum(tab, a, b, base_l + t), out_l, row, code_l, t)
        encode(own_sum(tab, a, b, base_l + PART + t) + decoded(in_l, scale_l, t), out_l, late, code_l, t + PART)
        return carry

    lax.fori_loop(0, PART, body, 0)
    write_codes(code_r, out_r, ROWS)
    write_codes(code_l, out_l, ROWS)


def middle_kernel(h, away, pos, tab, a, b, in_r, in_l, out_r, out_l, code_r, code_l, scale_r, scale_l):
    base_r = (pos[0] + away) % 8 * 32 + h * SUB
    base_l = (pos[0] + 8 - away) % 8 * 32 + h * SUB
    read_codes(in_r, ROWS, scale_r)
    read_codes(in_l, ROWS, scale_l)

    def body(g, carry):
        for u in range(2):
            t = g * 2 + u
            row = pl.multiple_of(t * TILE, TILE)
            encode(own_sum(tab, a, b, base_r + t) + decoded(in_r, scale_r, t), out_r, row, code_r, t)
            encode(own_sum(tab, a, b, base_l + t) + decoded(in_l, scale_l, t), out_l, row, code_l, t)
        return carry

    lax.fori_loop(0, SUB // 2, body, 0)
    write_codes(code_r, out_r, ROWS)
    write_codes(code_l, out_l, ROWS)


def own_kernel(pos, tab, a, b, own):
    def body(g, carry):
        for u in range(4):
            own[g * 4 + u] = own_sum(tab, a, b, pos[0] * 32 + g * 4 + u)
        return carry

    lax.fori_loop(0, own.shape[0] // 4, body, 0)


def final_sum(own, in_r, in_l, scale_r, scale_l, h, t):
    return own[h * SUB + t] + decoded(in_r, scale_r, t) + decoded(in_l, scale_l, t)


def put_block(sums, out, code):
    for n, one in enumerate(sums):
        encode(one, out, n * TILE, code, n)
    write_codes(code, out, len(sums) * TILE)


def spread_kernel(own, in_r, in_l, unused, far, up, down, code, scale_r, scale_l):
    read_codes(in_r, ROWS, scale_r)
    read_codes(in_l, ROWS, scale_l)
    code[...] = jnp.zeros_like(code)
    total = functools.partial(final_sum, own, in_r, in_l, scale_r, scale_l, 0)
    for k in range(2):
        put_block([total(4 * k + n) for n in range(4)], far.at[k], code.at[k])
        put_block([total(8 + 2 * k + n) for n in range(2)], up.at[k], code.at[2 + k])
        put_block([total(12 + 2 * k + n) for n in range(2)], down.at[k], code.at[4 + k])


def last_kernel(own, in_r, in_l, unused, up, down, cross, home, code, scale_r, scale_l):
    read_codes(in_r, ROWS, scale_r)
    read_codes(in_l, ROWS, scale_l)
    code[...] = jnp.zeros_like(code)
    total = functools.partial(final_sum, own, in_r, in_l, scale_r, scale_l, 1)
    for k in range(2):
        put_block([total(2 * k + n) for n in range(2)], up.at[k], code.at[k])
        put_block([total(4 + 2 * k + n) for n in range(2)], down.at[k], code.at[2 + k])
    put_block([total(12 + n) for n in range(4)], cross, code.at[4])
    for n in range(4):
        home[n] = total(8 + n)


def deliver_kernel(pos, far, up0, down0, up1, down1, swapped0, swapped1, cross, home, out, scale):
    col = pos[2]
    other = col + 1 - 2 * (col % 2)
    wide, slim = 4 * TILE + CODE_ROWS, 2 * TILE + CODE_ROWS

    def block(src, row, g, first, count):
        read_codes(src, row + count * TILE, scale)
        for n in range(count):
            rows = src[row + n * TILE : row + (n + 1) * TILE, :].astype(jnp.int32).astype(F32)
            out[(g + 8) % 8 * 4 + first + n] = rows * scale[n : n + 1, :]

    block(far.at[0], 0, col + 4, 0, 4)
    block(up0.at[0], 0, col - 2, 0, 2)
    block(down0.at[0], 0, col + 2, 0, 2)
    block(swapped0, 0, other + 4, 0, 4)
    block(swapped0, wide, other - 2, 0, 2)
    block(swapped0, wide + slim, other + 2, 0, 2)
    block(up1.at[0], 0, col - 2, 2, 2)
    block(down1.at[0], 0, col + 2, 2, 2)
    block(swapped1, 0, other - 2, 2, 2)
    block(swapped1, slim, other + 2, 2, 2)
    block(cross, 0, other, 0, 4)
    for n in range(4):
        out[col * 4 + n] = home[n]


SMEM_SPEC = pl.BlockSpec(memory_space=pltpu.SMEM)
VMEM_SPEC = pl.BlockSpec(memory_space=pltpu.VMEM)
ANY_SPEC = pl.BlockSpec(memory_space=pl.ANY)


def params(mib):
    return pltpu.CompilerParams(vmem_limit_bytes=mib * 2**20)


COST_FIRST = 2
COST_SECOND0 = 3
COST_SECOND1 = 3
COST_MIDDLE = 3
COST_OWN = 3
COST_LAST = 1


def cost(us):
    return pl.CostEstimate(flops=int(us * 1e9), bytes_accessed=int(us * 3e6), transcendentals=0)


def scratch(count):
    return [pltpu.VMEM((CODE_ROWS, TILE), F32)] * count


def message(rows):
    return jax.ShapeDtypeStruct((rows + CODE_ROWS, TILE), I16)


def step(kernel, name, weight, out_shape, scratches, after, *args):
    ins = [SMEM_SPEC, SMEM_SPEC] + [VMEM_SPEC] * (len(args) - 2) + [ANY_SPEC]
    count = len(args)

    def body(*refs):
        kernel(*refs[:count], *refs[count + 1 :])

    return pl.pallas_call(
        body,
        out_shape=out_shape,
        in_specs=ins,
        out_specs=jax.tree.map(lambda _: VMEM_SPEC, out_shape),
        scratch_shapes=scratch(scratches),
        compiler_params=params(16),
        cost_estimate=cost(weight),
        name=name,
    )(*args, after)


def own_tiles(after, *args):
    def body(pos, tab, a, b, unused, own):
        own_kernel(pos, tab, a, b, own)

    return pl.pallas_call(
        body,
        out_shape=VM((2 * SUB, TILE, TILE), F32),
        in_specs=[SMEM_SPEC] * 2 + [VMEM_SPEC] * 2 + [ANY_SPEC],
        out_specs=VMEM_SPEC,
        compiler_params=params(16),
        cost_estimate=cost(COST_OWN),
        name="own",
    )(*args, after)


def coded(tiles, *lead):
    return jax.ShapeDtypeStruct(lead + (tiles * TILE + CODE_ROWS, TILE), I16)


def finals(kernel, name, out_shape, after, *args):
    return pl.pallas_call(
        kernel,
        out_shape=out_shape,
        in_specs=[VMEM_SPEC] * 3 + [ANY_SPEC],
        out_specs=(VMEM_SPEC,) * len(out_shape),
        scratch_shapes=[pltpu.VMEM((6, CODE_ROWS, TILE), F32)] + scratch(2),
        compiler_params=params(16),
        cost_estimate=cost(COST_LAST),
        name=name,
    )(*args, after)


def deliver(tiles, *args):
    return pl.pallas_call(
        deliver_kernel,
        out_shape=jax.ShapeDtypeStruct((tiles, TILE, TILE), F32),
        in_specs=[SMEM_SPEC] + [VMEM_SPEC] * (len(args) - 1),
        out_specs=VMEM_SPEC,
        scratch_shapes=scratch(1),
        compiler_params=params(16),
        cost_estimate=cost(COST_LAST),
        name="deliver",
    )(*args)


def in_hbm(x):
    return pltpu.with_memory_space_constraint(x, pltpu.HBM)


def per_device(a_tiles, a_kcol, b_tiles, b_jcol, c_jcol, c_place):
    depth, row, col = (lax.axis_size(n) for n in ("depth", "row", "col"))

    def shift(axis, size, by):
        pairs = [(i, (i + by) % size) for i in range(size)]
        return lambda x: lax.ppermute(x, axis, pairs)

    def x_split(x):
        return lax.ppermute(x, "col", [(i, (i + 2 - 4 * (i % 2)) % col) for i in range(col)])

    def y_split(x):
        pairs = []
        for r in range(row):
            for c in range(col):
                pairs.append((r * col + c, (r + 1 - 2 * (c % 2)) % row * col + c))
        return lax.ppermute(x, ("row", "col"), pairs)

    z_up, z_down = shift("depth", depth, 1), shift("depth", depth, -1)

    def swap(x):
        return lax.ppermute(x, "col", [(i, i ^ 1) for i in range(col)])

    pos = jnp.stack([lax.axis_index(n) for n in ("depth", "row", "col")]).astype(jnp.int32)
    b0 = b_tiles.reshape((-1,) + b_tiles.shape[2:])
    a0 = a_tiles.reshape((-1,) + a_tiles.shape[2:])
    q1, p1 = y_split(b0), x_split(a0)
    bp, ap = swap(b0), swap(a0)
    q2, p2 = y_split(bp), x_split(ap)
    q3, p3 = y_split(q1), x_split(p1)
    t2, s1, s2, s3 = swap(q2), swap(p1), swap(p2), swap(p3)
    tab = make_table(a_kcol, b_jcol, c_jcol, c_place)
    b_vmem = VM((b0.shape[0] + 1, TILE, TILE), BF16)
    a, b = pl.pallas_call(
        assemble_kernel,
        out_shape=(VM((a0.shape[0], TILE, TILE), BF16), b_vmem),
        in_specs=[SMEM_SPEC] + [ANY_SPEC] * 11,
        out_specs=(VMEM_SPEC, VMEM_SPEC),
        scratch_shapes=[pltpu.SemaphoreType.DMA((11,))],
        compiler_params=params(16),
        cost_estimate=cost(0),
        name="assemble",
    )(pos, in_hbm(a0), ap, p1, p2, p3, s1, s2, s3, in_hbm(b0), q1, t2)

    short = (message(HALF_ROWS),) * 2
    full = (message(ROWS),) * 2
    flying = []
    for h in range(2):
        if h == 0:
            r, l, b = pl.pallas_call(
                finish_kernel,
                out_shape=short + (b_vmem,),
                in_specs=[SMEM_SPEC] * 2 + [VMEM_SPEC] * 2 + [ANY_SPEC],
                out_specs=(VMEM_SPEC,) * 3,
                scratch_shapes=scratch(2) + [pltpu.SemaphoreType.DMA],
                input_output_aliases={3: 2},
                compiler_params=params(16),
                cost_estimate=cost(COST_FIRST),
                name="first0",
            )(pos, tab, a, b, q3)
        else:
            r, l = step(functools.partial(first_kernel, h), f"first{h}", COST_FIRST, short, 2, r, pos, tab, a, b)
        flying.append((z_up(r), z_down(l)))
    for hop in range(3):
        landed, flying = flying, []
        for h in range(2):
            if hop == 0:
                kernel, name = functools.partial(second_kernel, h), f"second{h}"
            else:
                kernel, name = functools.partial(middle_kernel, h, 3 - hop), f"middle{hop}{h}"
            weight = (COST_SECOND0, COST_SECOND1)[h] if hop == 0 else COST_MIDDLE
            r, l = step(kernel, name, weight, full, 4, r, pos, tab, a, b, *landed[h])
            flying.append((z_up(r), z_down(l)))
    own = own_tiles(r, pos, tab, a, b)
    x_up, x_down, x_far = (shift("col", col, n) for n in (2, -2, 4))
    far, up, down = finals(spread_kernel, "spread", (coded(4, 2), coded(2, 2), coded(2, 2)), r, own, *flying[0])
    far, up, down = x_far(far), x_up(up), x_down(down)
    up1, down1, cross, home = finals(
        last_kernel,
        "last",
        (coded(2, 2), coded(2, 2), coded(4), jax.ShapeDtypeStruct((4, TILE, TILE), F32)),
        up,
        own,
        *flying[1],
    )
    up1, down1, cross = x_up(up1), x_down(down1), swap(cross)
    swapped = swap(jnp.concatenate([far[1], up[1], down[1]]))
    swapped1 = swap(jnp.concatenate([up1[1], down1[1]]))
    return deliver(col * 4, pos, far, up, down, up1, down1, swapped, swapped1, cross, home)


def solution(mesh):
    return jax.shard_map(
        per_device,
        mesh=mesh,
        in_specs=(
            P("row", "depth", "col", None),
            P("row", "depth"),
            P("depth", "col", "row", None),
            P("depth", "col"),
            P("row", "col"),
            P("row", "col"),
        ),
        out_specs=P(("depth", "row", "col"), None, None),
        check_vma=False,
    )
```

```python
import functools

import jax
import jax.numpy as jnp
from jax import lax
from jax.experimental import pallas as pl
from jax.experimental.pallas import tpu as pltpu
from jax.sharding import PartitionSpec as P

F32 = jnp.float32
I16 = jnp.int16
BF16 = jnp.bfloat16
VM = pltpu.VMEM
TOP = 32767.0
FINE = 128.0
TINY = 2.0**-110
TILE = 128
PART = 8
SUB = 16
ROWS = SUB * TILE
HALF_ROWS = PART * TILE
CODE_ROWS = 16


def select_blocks(a_kcol, b_jcol, c_jcol):
    k_rows, b_count = b_jcol.shape
    k_ids = jnp.arange(k_rows, dtype=jnp.int32)
    onehot_k = (a_kcol[:, :, None] == k_ids[None, None, :]).astype(jnp.int32)
    tile_cols = jnp.sum(onehot_k[:, :, :, None] * b_jcol[None, None, :, :], axis=2)
    matches = tile_cols[:, None, :, :] == c_jcol[:, :, None, None]
    slot_ids = jnp.arange(b_count, dtype=jnp.int32)
    chosen = jnp.sum(jnp.where(matches, slot_ids[None, None, None, :], 0), axis=3)
    located = jnp.any(matches, axis=3)
    flat_index = a_kcol[:, None, :] * b_count + chosen
    return jnp.where(located, flat_index, k_rows * b_count)


ORDER = (
    [(2, k, j) for k in range(2) for j in range(4)]
    + [(d, k, j) for d in (1, 3) for k in range(2) for j in (0, 1)]
    + [(d, k, j) for d in (1, 3) for k in range(2) for j in (2, 3)]
    + [(0, k, j) for k in range(2) for j in range(4)]
)


def make_table(a_kcol, b_jcol, c_jcol, c_place):
    col = lax.axis_index("col")
    away, core, tile = (jnp.array([entry[n] for entry in ORDER], jnp.int32) for n in range(3))
    owner = (col // 2 + away) % 4 * 2 + (col + core) % 2
    picks = select_blocks(a_kcol, b_jcol, c_jcol)
    rows, kept, slots = picks.shape
    row_ids = jnp.broadcast_to(jnp.arange(rows, dtype=jnp.int32)[:, None, None], (rows, kept, 1))
    fields = jnp.concatenate([row_ids, picks], axis=2).reshape(rows * kept, slots + 1)
    q = jnp.arange(rows * kept, dtype=jnp.int32)
    target = q // 32 * 32 + jnp.tile(owner * 4 + tile, rows * kept // 32)
    hit = c_place.reshape(1, rows * kept) == target[:, None]
    table = jnp.sum(jnp.where(hit[:, :, None], fields[None], 0), axis=1)
    return table.reshape(rows * kept * (slots + 1))


def a_place(a_out, col):
    return a_out.at[:, pl.ds(pl.multiple_of((col + 8) % 8 * 16, 16), 16), :]


def b_place(b_out, row, count):
    return b_out.at[pl.ds(0, count), pl.ds(pl.multiple_of(row % 4 * 32, 32), 32), :]


def copy_all(copies, sem):
    started = [pltpu.make_async_copy(src, dst, sem.at[n]) for n, (src, dst) in enumerate(copies)]
    for one in started:
        one.start()
    return started


def assemble_kernel(pos, a0, ap, p1, p2, p3, s1, b0, q1, t2, a_out, b_out, sem):
    row, col = pos[1], pos[2]
    core = col % 2
    other = col + 1 - 2 * core
    ahead = 4 * core - 2
    count = b0.shape[0]
    copies = [
        (a0, a_place(a_out, col)),
        (ap, a_place(a_out, other)),
        (p1, a_place(a_out, col + ahead)),
        (p2, a_place(a_out, other + ahead)),
        (p3, a_place(a_out, col + 4)),
        (s1, a_place(a_out, other - ahead)),
        (b0, b_place(b_out, row, count)),
        (q1, b_place(b_out, row + 3 + 2 * core, count)),
        (t2, b_place(b_out, row + 1 + 2 * core, count)),
    ]
    started = copy_all(copies, sem)
    b_out[count] = jnp.zeros(b_out.shape[1:], BF16)
    for one in started:
        one.wait()


def own_sum(tab, a, b, q):
    base = q * 6
    i = tab[base]
    left = jnp.concatenate([a[i * 5 + s] for s in range(5)], axis=1)
    right = jnp.concatenate([b[tab[base + 1 + s]] for s in range(5)], axis=0)
    return jnp.dot(left, right, preferred_element_type=F32)


def read_codes(ref, row, scale):
    codes = ref[pl.ds(row, CODE_ROWS), :].astype(jnp.int32).astype(F32)
    scale[...] = jnp.exp2(codes * (1.0 / FINE)) * (1.0 / TOP)


def decoded(ref, scale, t):
    rows = ref[pl.ds(pl.multiple_of(t * TILE, TILE), TILE), :]
    return rows.astype(jnp.int32).astype(F32) * scale[pl.ds(t, 1), :]


def encode(acc, out, row, codes, t):
    top = jnp.maximum(jnp.max(jnp.abs(acc), axis=0, keepdims=True), TINY)
    code = jnp.ceil(jnp.log2(top) * FINE) + 1.0
    codes[pl.ds(t, 1), :] = code
    quant = jnp.round(acc * (jnp.exp2(code * (-1.0 / FINE)) * TOP))
    out[pl.ds(row, TILE), :] = quant.astype(jnp.int32).astype(I16)


def write_codes(codes, out, row):
    out[pl.ds(row, CODE_ROWS), :] = codes[...].astype(jnp.int32).astype(I16)


def finish_kernel(pos, tab, a_in, b_in, s2, s3, q3, out_r, out_l, a, b, code_r, code_l, sem):
    row, col = pos[1], pos[2]
    core = col % 2
    copies = [
        (s2, a_place(a, col + 2 - 4 * core)),
        (s3, a_place(a, col + 5 - 2 * core)),
        (q3, b_place(b, row + 2, q3.shape[0])),
    ]
    for one in copy_all(copies, sem):
        one.wait()
    first_kernel(0, pos, tab, a, b, out_r, out_l, code_r, code_l)


def first_kernel(h, pos, tab, a, b, out_r, out_l, code_r, code_l):
    base = (pos[0] + 4) % 8 * 32 + h * SUB
    code_r[...] = jnp.zeros_like(code_r)
    code_l[...] = jnp.zeros_like(code_l)

    def body(g, carry):
        places = [g * 4 + u for u in range(4)]
        sums = [(own_sum(tab, a, b, base + t), own_sum(tab, a, b, base + PART + t)) for t in places]
        for t, (r, l) in zip(places, sums):
            row = pl.multiple_of(t * TILE, TILE)
            encode(r, out_r, row, code_r, t)
            encode(l, out_l, row, code_l, t)
        return carry

    lax.fori_loop(0, PART // 4, body, 0)
    write_codes(code_r, out_r, HALF_ROWS)
    write_codes(code_l, out_l, HALF_ROWS)


def second_kernel(h, pos, tab, a, b, in_r, in_l, out_r, out_l, code_r, code_l, scale_r, scale_l):
    base_r = (pos[0] + 3) % 8 * 32 + h * SUB
    base_l = (pos[0] + 5) % 8 * 32 + h * SUB
    read_codes(in_r, HALF_ROWS, scale_r)
    read_codes(in_l, HALF_ROWS, scale_l)

    def body(g, carry):
        places = [g * 2 + u for u in range(2)]
        sums = []
        for t in places:
            sums.append([own_sum(tab, a, b, q + t) for q in (base_r, base_r + PART, base_l, base_l + PART)])
        for t, (r, late_r, l, late_l) in zip(places, sums):
            row = pl.multiple_of(t * TILE, TILE)
            late = pl.multiple_of((t + PART) * TILE, TILE)
            encode(r + decoded(in_r, scale_r, t), out_r, row, code_r, t)
            encode(late_r, out_r, late, code_r, t + PART)
            encode(l, out_l, row, code_l, t)
            encode(late_l + decoded(in_l, scale_l, t), out_l, late, code_l, t + PART)
        return carry

    lax.fori_loop(0, PART // 2, body, 0)
    write_codes(code_r, out_r, ROWS)
    write_codes(code_l, out_l, ROWS)


def middle_kernel(h, away, pos, tab, a, b, in_r, in_l, out_r, out_l, code_r, code_l, scale_r, scale_l):
    base_r = (pos[0] + away) % 8 * 32 + h * SUB
    base_l = (pos[0] + 8 - away) % 8 * 32 + h * SUB
    read_codes(in_r, ROWS, scale_r)
    read_codes(in_l, ROWS, scale_l)

    def body(g, carry):
        places = [g * 4 + u for u in range(4)]
        sums = [(own_sum(tab, a, b, base_r + t), own_sum(tab, a, b, base_l + t)) for t in places]
        for t, (r, l) in zip(places, sums):
            row = pl.multiple_of(t * TILE, TILE)
            encode(r + decoded(in_r, scale_r, t), out_r, row, code_r, t)
            encode(l + decoded(in_l, scale_l, t), out_l, row, code_l, t)
        return carry

    lax.fori_loop(0, SUB // 4, body, 0)
    write_codes(code_r, out_r, ROWS)
    write_codes(code_l, out_l, ROWS)


def own_kernel(pos, tab, a, b, own):
    def body(g, carry):
        sums = [own_sum(tab, a, b, pos[0] * 32 + g * 8 + u) for u in range(8)]
        for u, one in enumerate(sums):
            own[g * 8 + u] = one
        return carry

    lax.fori_loop(0, own.shape[0] // 8, body, 0)


def final_sum(own, in_r, in_l, scale_r, scale_l, h, t):
    return own[h * SUB + t] + decoded(in_r, scale_r, t) + decoded(in_l, scale_l, t)


def put_block(sums, out, code):
    for n, one in enumerate(sums):
        encode(one, out, n * TILE, code, n)
    write_codes(code, out, len(sums) * TILE)


def spread_kernel(own, in_r, in_l, unused, far, up, down, code, scale_r, scale_l):
    read_codes(in_r, ROWS, scale_r)
    read_codes(in_l, ROWS, scale_l)
    code[...] = jnp.zeros_like(code)
    total = functools.partial(final_sum, own, in_r, in_l, scale_r, scale_l, 0)
    for k in range(2):
        put_block([total(4 * k + n) for n in range(4)], far.at[k], code.at[k])
        put_block([total(8 + 2 * k + n) for n in range(2)], up.at[k], code.at[2 + k])
        put_block([total(12 + 2 * k + n) for n in range(2)], down.at[k], code.at[4 + k])


def last_kernel(own, in_r, in_l, unused, up, down, cross, home, code, scale_r, scale_l):
    read_codes(in_r, ROWS, scale_r)
    read_codes(in_l, ROWS, scale_l)
    code[...] = jnp.zeros_like(code)
    total = functools.partial(final_sum, own, in_r, in_l, scale_r, scale_l, 1)
    for k in range(2):
        put_block([total(2 * k + n) for n in range(2)], up.at[k], code.at[k])
        put_block([total(4 + 2 * k + n) for n in range(2)], down.at[k], code.at[2 + k])
    put_block([total(12 + n) for n in range(4)], cross, code.at[4])
    for n in range(4):
        home[n] = total(8 + n)


def deliver_blocks(blocks, out, tiles, scale, sem):
    started, at = [], 0
    for n, (src, row, g, first, count) in enumerate(blocks):
        read_codes(src, row + count * TILE, scale)
        for m in range(count):
            rows = src[row + m * TILE : row + (m + 1) * TILE, :].astype(jnp.int32).astype(F32)
            tiles[at + m] = rows * scale[m : m + 1, :]
        to = out.at[pl.ds((g + 8) % 8 * 4 + first, count)]
        started.append(pltpu.make_async_copy(tiles.at[pl.ds(at, count)], to, sem.at[n]))
        started[-1].start()
        at += count
    return started


WIDE, SLIM = 4 * TILE + CODE_ROWS, 2 * TILE + CODE_ROWS


def deliver_early_kernel(pos, far, up, down, swapped, home, out, tiles, scale, sem):
    col = pos[2]
    other = col + 1 - 2 * (col % 2)
    blocks = [
        (far.at[0], 0, col + 4, 0, 4),
        (up.at[0], 0, col - 2, 0, 2),
        (down.at[0], 0, col + 2, 0, 2),
        (swapped, 0, other + 4, 0, 4),
        (swapped, WIDE, other - 2, 0, 2),
        (swapped, WIDE + SLIM, other + 2, 0, 2),
    ]
    kept = pltpu.make_async_copy(home, out.at[pl.ds(col * 4, 4)], sem.at[len(blocks)])
    kept.start()
    for one in deliver_blocks(blocks, out, tiles, scale, sem) + [kept]:
        one.wait()


def deliver_late_kernel(pos, early, up, down, swapped, cross, out, tiles, scale, sem):
    col = pos[2]
    other = col + 1 - 2 * (col % 2)
    blocks = [
        (cross, 0, other, 0, 4),
        (up.at[0], 0, col - 2, 2, 2),
        (down.at[0], 0, col + 2, 2, 2),
        (swapped, 0, other - 2, 2, 2),
        (swapped, SLIM, other + 2, 2, 2),
    ]
    for one in deliver_blocks(blocks, out, tiles, scale, sem):
        one.wait()


SMEM_SPEC = pl.BlockSpec(memory_space=pltpu.SMEM)
VMEM_SPEC = pl.BlockSpec(memory_space=pltpu.VMEM)
ANY_SPEC = pl.BlockSpec(memory_space=pl.ANY)


def params(mib):
    return pltpu.CompilerParams(vmem_limit_bytes=mib * 2**20)


COST_FIRST = 2
COST_SECOND0 = 3
COST_SECOND1 = 3
COST_MIDDLE = 3
COST_OWN = 3
COST_LAST = 1


def cost(us):
    return pl.CostEstimate(flops=int(us * 1e9), bytes_accessed=int(us * 3e6), transcendentals=0)


def scratch(count):
    return [pltpu.VMEM((CODE_ROWS, TILE), F32)] * count


def message(rows):
    return jax.ShapeDtypeStruct((rows + CODE_ROWS, TILE), I16)


def step(kernel, name, weight, out_shape, scratches, after, *args):
    ins = [SMEM_SPEC, SMEM_SPEC] + [VMEM_SPEC] * (len(args) - 2) + [ANY_SPEC]
    count = len(args)

    def body(*refs):
        kernel(*refs[:count], *refs[count + 1 :])

    return pl.pallas_call(
        body,
        out_shape=out_shape,
        in_specs=ins,
        out_specs=jax.tree.map(lambda _: VMEM_SPEC, out_shape),
        scratch_shapes=scratch(scratches),
        compiler_params=params(16),
        cost_estimate=cost(weight),
        name=name,
    )(*args, after)


def own_tiles(after, *args):
    def body(pos, tab, a, b, unused, own):
        own_kernel(pos, tab, a, b, own)

    return pl.pallas_call(
        body,
        out_shape=VM((2 * SUB, TILE, TILE), F32),
        in_specs=[SMEM_SPEC] * 2 + [VMEM_SPEC] * 2 + [ANY_SPEC],
        out_specs=VMEM_SPEC,
        compiler_params=params(16),
        cost_estimate=cost(COST_OWN),
        name="own",
    )(*args, after)


def coded(tiles, *lead):
    return jax.ShapeDtypeStruct(lead + (tiles * TILE + CODE_ROWS, TILE), I16)


def finals(kernel, name, out_shape, after, *args):
    return pl.pallas_call(
        kernel,
        out_shape=out_shape,
        in_specs=[VMEM_SPEC] * 3 + [ANY_SPEC],
        out_specs=(VMEM_SPEC,) * len(out_shape),
        scratch_shapes=[pltpu.VMEM((6, CODE_ROWS, TILE), F32)] + scratch(2),
        compiler_params=params(16),
        cost_estimate=cost(COST_LAST),
        name=name,
    )(*args, after)


def deliver(kernel, name, specs, tiles, moved, aliases, *args):
    return pl.pallas_call(
        kernel,
        out_shape=jax.ShapeDtypeStruct((tiles, TILE, TILE), F32),
        in_specs=[SMEM_SPEC] + specs,
        out_specs=ANY_SPEC,
        scratch_shapes=[pltpu.VMEM((moved, TILE, TILE), F32)] + scratch(1) + [pltpu.SemaphoreType.DMA((7,))],
        input_output_aliases=aliases,
        compiler_params=params(16),
        cost_estimate=cost(COST_LAST),
        name=name,
    )(*args)


def in_hbm(x):
    return pltpu.with_memory_space_constraint(x, pltpu.HBM)


def per_device(a_tiles, a_kcol, b_tiles, b_jcol, c_jcol, c_place):
    depth, row, col = (lax.axis_size(n) for n in ("depth", "row", "col"))

    def shift(axis, size, by):
        pairs = [(i, (i + by) % size) for i in range(size)]
        return lambda x: lax.ppermute(x, axis, pairs)

    def x_split(x):
        return lax.ppermute(x, "col", [(i, (i + 2 - 4 * (i % 2)) % col) for i in range(col)])

    def y_split(x):
        pairs = []
        for r in range(row):
            for c in range(col):
                pairs.append((r * col + c, (r + 1 - 2 * (c % 2)) % row * col + c))
        return lax.ppermute(x, ("row", "col"), pairs)

    z_up, z_down = shift("depth", depth, 1), shift("depth", depth, -1)

    def swap(x):
        return lax.ppermute(x, "col", [(i, i ^ 1) for i in range(col)])

    pos = jnp.stack([lax.axis_index(n) for n in ("depth", "row", "col")]).astype(jnp.int32)
    b0 = b_tiles.reshape((-1,) + b_tiles.shape[2:])
    a0 = a_tiles.reshape((-1,) + a_tiles.shape[2:])
    q1, p1 = y_split(b0), x_split(a0)
    bp, ap = swap(b0), swap(a0)
    q2, p2 = y_split(bp), x_split(ap)
    q3, p3 = y_split(q1), x_split(p1)
    t2, s1, s2, s3 = swap(q2), swap(p1), swap(p2), swap(p3)
    tab = make_table(a_kcol, b_jcol, c_jcol, c_place)
    held = (VM((a0.shape[0], TILE, TILE), BF16), VM((b0.shape[0] + 1, TILE, TILE), BF16))
    a, b = pl.pallas_call(
        assemble_kernel,
        out_shape=held,
        in_specs=[SMEM_SPEC] + [ANY_SPEC] * 9,
        out_specs=(VMEM_SPEC, VMEM_SPEC),
        scratch_shapes=[pltpu.SemaphoreType.DMA((9,))],
        compiler_params=params(16),
        cost_estimate=cost(0),
        name="assemble",
    )(pos, in_hbm(a0), ap, p1, p2, p3, s1, in_hbm(b0), q1, t2)

    short = (message(HALF_ROWS),) * 2
    full = (message(ROWS),) * 2
    flying = []
    for h in range(2):
        if h == 0:
            r, l, a, b = pl.pallas_call(
                finish_kernel,
                out_shape=short + held,
                in_specs=[SMEM_SPEC] * 2 + [VMEM_SPEC] * 2 + [ANY_SPEC] * 3,
                out_specs=(VMEM_SPEC,) * 4,
                scratch_shapes=scratch(2) + [pltpu.SemaphoreType.DMA((3,))],
                input_output_aliases={2: 2, 3: 3},
                compiler_params=params(16),
                cost_estimate=cost(COST_FIRST),
                name="first0",
            )(pos, tab, a, b, s2, s3, q3)
        else:
            r, l = step(functools.partial(first_kernel, h), f"first{h}", COST_FIRST, short, 2, r, pos, tab, a, b)
        flying.append((z_up(r), z_down(l)))
    for hop in range(3):
        landed, flying = flying, []
        for h in range(2):
            if (hop, h) == (2, 1):
                own = r = own_tiles(r, pos, tab, a, b)
            if hop == 0:
                kernel, name = functools.partial(second_kernel, h), f"second{h}"
            else:
                kernel, name = functools.partial(middle_kernel, h, 3 - hop), f"middle{hop}{h}"
            weight = (COST_SECOND0, COST_SECOND1)[h] if hop == 0 else COST_MIDDLE
            r, l = step(kernel, name, weight, full, 4, r, pos, tab, a, b, *landed[h])
            flying.append((z_up(r), z_down(l)))
    x_up, x_down, x_far = (shift("col", col, n) for n in (2, -2, 4))
    far, up, down = finals(spread_kernel, "spread", (coded(4, 2), coded(2, 2), coded(2, 2)), r, own, *flying[0])
    far, up, down = x_far(far), x_up(up), x_down(down)
    up1, down1, cross, home = finals(
        last_kernel,
        "last",
        (coded(2, 2), coded(2, 2), coded(4), jax.ShapeDtypeStruct((4, TILE, TILE), F32)),
        up,
        own,
        *flying[1],
    )
    up1, down1, cross = x_up(up1), x_down(down1), swap(cross)
    far, down, home = lax.optimization_barrier((far, down, home))
    swapped = swap(jnp.concatenate([far[1], up[1], down[1]]))
    early = deliver(
        deliver_early_kernel, "deliver0", [VMEM_SPEC] * 5, col * 4, 16, {}, pos, far, up, down, swapped, home
    )
    swapped1 = swap(jnp.concatenate([up1[1], down1[1]]))
    return deliver(
        deliver_late_kernel,
        "deliver1",
        [ANY_SPEC] + [VMEM_SPEC] * 4,
        col * 4,
        12,
        {1: 0},
        pos,
        early,
        up1,
        down1,
        swapped1,
        cross,
    )


def solution(mesh):
    return jax.shard_map(
        per_device,
        mesh=mesh,
        in_specs=(
            P("row", "depth", "col", None),
            P("row", "depth"),
            P("depth", "col", "row", None),
            P("depth", "col"),
            P("row", "col"),
            P("row", "col"),
        ),
        out_specs=P(("depth", "row", "col"), None, None),
        check_vma=False,
    )
```

```python
import functools

import jax
import jax.numpy as jnp
from jax import lax
from jax.experimental import pallas as pl
from jax.experimental.pallas import tpu as pltpu
from jax.sharding import PartitionSpec as P

F32 = jnp.float32
I16 = jnp.int16
BF16 = jnp.bfloat16
VM = pltpu.VMEM
TOP = 32767.0
FINE = 128.0
TINY = 2.0**-110
TILE = 128
PART = 8
SUB = 16
ROWS = SUB * TILE
HALF_ROWS = PART * TILE
CODE_ROWS = 16


def select_blocks(a_kcol, b_jcol, c_jcol):
    k_rows, b_count = b_jcol.shape
    k_ids = jnp.arange(k_rows, dtype=jnp.int32)
    onehot_k = (a_kcol[:, :, None] == k_ids[None, None, :]).astype(jnp.int32)
    tile_cols = jnp.sum(onehot_k[:, :, :, None] * b_jcol[None, None, :, :], axis=2)
    matches = tile_cols[:, None, :, :] == c_jcol[:, :, None, None]
    slot_ids = jnp.arange(b_count, dtype=jnp.int32)
    chosen = jnp.sum(jnp.where(matches, slot_ids[None, None, None, :], 0), axis=3)
    located = jnp.any(matches, axis=3)
    flat_index = a_kcol[:, None, :] * b_count + chosen
    return jnp.where(located, flat_index, k_rows * b_count)


ORDER = (
    [(2, k, j) for k in range(2) for j in range(4)]
    + [(d, k, j) for d in (1, 3) for k in range(2) for j in (0, 1)]
    + [(d, k, j) for d in (1, 3) for k in range(2) for j in (2, 3)]
    + [(0, k, j) for k in range(2) for j in range(4)]
)


def make_table(a_kcol, b_jcol, c_jcol, c_place):
    col = lax.axis_index("col")
    away, core, tile = (jnp.array([entry[n] for entry in ORDER], jnp.int32) for n in range(3))
    owner = (col // 2 + away) % 4 * 2 + (col + core) % 2
    picks = select_blocks(a_kcol, b_jcol, c_jcol)
    rows, kept, slots = picks.shape
    row_ids = jnp.broadcast_to(jnp.arange(rows, dtype=jnp.int32)[:, None, None], (rows, kept, 1))
    fields = jnp.concatenate([row_ids, picks], axis=2).reshape(rows * kept, slots + 1)
    q = jnp.arange(rows * kept, dtype=jnp.int32)
    target = q // 32 * 32 + jnp.tile(owner * 4 + tile, rows * kept // 32)
    hit = c_place.reshape(1, rows * kept) == target[:, None]
    table = jnp.sum(jnp.where(hit[:, :, None], fields[None], 0), axis=1)
    return table.reshape(rows * kept * (slots + 1))


def a_place(a_out, col):
    return a_out.at[:, pl.ds(pl.multiple_of((col + 8) % 8 * 16, 16), 16), :]


def b_place(b_out, row, count):
    return b_out.at[pl.ds(0, count), pl.ds(pl.multiple_of(row % 4 * 32, 32), 32), :]


def copy_all(copies, sem):
    started = [pltpu.make_async_copy(src, dst, sem.at[n]) for n, (src, dst) in enumerate(copies)]
    for one in started:
        one.start()
    return started


def assemble_kernel(pos, a0, ap, p1, p2, p3, s1, b0, q1, t2, a_out, b_out, sem):
    row, col = pos[1], pos[2]
    core = col % 2
    other = col + 1 - 2 * core
    ahead = 4 * core - 2
    count = b0.shape[0]
    copies = [
        (a0, a_place(a_out, col)),
        (ap, a_place(a_out, other)),
        (p1, a_place(a_out, col + ahead)),
        (p2, a_place(a_out, other + ahead)),
        (p3, a_place(a_out, col + 4)),
        (s1, a_place(a_out, other - ahead)),
        (b0, b_place(b_out, row, count)),
        (q1, b_place(b_out, row + 3 + 2 * core, count)),
        (t2, b_place(b_out, row + 1 + 2 * core, count)),
    ]
    started = copy_all(copies, sem)
    b_out[count] = jnp.zeros(b_out.shape[1:], BF16)
    for one in started:
        one.wait()


def own_sum(tab, a, b, q):
    base = q * 6
    i = tab[base]
    left = jnp.concatenate([a[i * 5 + s] for s in range(5)], axis=1)
    right = jnp.concatenate([b[tab[base + 1 + s]] for s in range(5)], axis=0)
    return jnp.dot(left, right, preferred_element_type=F32)


def read_codes(ref, row, scale):
    codes = ref[pl.ds(row, CODE_ROWS), :].astype(jnp.int32).astype(F32)
    scale[...] = jnp.exp2(codes * (1.0 / FINE)) * (1.0 / TOP)


def decoded(ref, scale, t):
    rows = ref[pl.ds(pl.multiple_of(t * TILE, TILE), TILE), :]
    return rows.astype(jnp.int32).astype(F32) * scale[pl.ds(t, 1), :]


def encode(acc, out, row, codes, t):
    top = jnp.maximum(jnp.max(jnp.abs(acc), axis=0, keepdims=True), TINY)
    code = jnp.ceil(jnp.log2(top) * FINE) + 1.0
    codes[pl.ds(t, 1), :] = code
    quant = jnp.round(acc * (jnp.exp2(code * (-1.0 / FINE)) * TOP))
    out[pl.ds(row, TILE), :] = quant.astype(jnp.int32).astype(I16)


def write_codes(codes, out, row):
    out[pl.ds(row, CODE_ROWS), :] = codes[...].astype(jnp.int32).astype(I16)


def finish_kernel(pos, tab, a_in, b_in, s2, s3, q3, out_r, out_l, a, b, code_r, code_l, sem):
    row, col = pos[1], pos[2]
    core = col % 2
    copies = [
        (s2, a_place(a, col + 2 - 4 * core)),
        (s3, a_place(a, col + 5 - 2 * core)),
        (q3, b_place(b, row + 2, q3.shape[0])),
    ]
    for one in copy_all(copies, sem):
        one.wait()
    first_kernel(0, pos, tab, a, b, out_r, out_l, code_r, code_l)


def first_kernel(h, pos, tab, a, b, out_r, out_l, code_r, code_l):
    base = (pos[0] + 4) % 8 * 32 + h * SUB
    code_r[...] = jnp.zeros_like(code_r)
    code_l[...] = jnp.zeros_like(code_l)

    def body(g, carry):
        places = [g * 4 + u for u in range(4)]
        sums = [(own_sum(tab, a, b, base + t), own_sum(tab, a, b, base + PART + t)) for t in places]
        for t, (r, l) in zip(places, sums):
            row = pl.multiple_of(t * TILE, TILE)
            encode(r, out_r, row, code_r, t)
            encode(l, out_l, row, code_l, t)
        return carry

    lax.fori_loop(0, PART // 4, body, 0)
    write_codes(code_r, out_r, HALF_ROWS)
    write_codes(code_l, out_l, HALF_ROWS)


def second_kernel(h, pos, tab, a, b, in_r, in_l, out_r, out_l, code_r, code_l, scale_r, scale_l):
    base_r = (pos[0] + 5) % 8 * 32 + h * SUB
    base_l = (pos[0] + 3) % 8 * 32 + h * SUB
    read_codes(in_r, HALF_ROWS, scale_r)
    read_codes(in_l, HALF_ROWS, scale_l)

    def body(g, carry):
        places = [g * 2 + u for u in range(2)]
        sums = []
        for t in places:
            sums.append([own_sum(tab, a, b, q + t) for q in (base_r, base_r + PART, base_l, base_l + PART)])
        for t, (r, late_r, l, late_l) in zip(places, sums):
            row = pl.multiple_of(t * TILE, TILE)
            late = pl.multiple_of((t + PART) * TILE, TILE)
            encode(r + decoded(in_r, scale_r, t), out_r, row, code_r, t)
            encode(late_r, out_r, late, code_r, t + PART)
            encode(l, out_l, row, code_l, t)
            encode(late_l + decoded(in_l, scale_l, t), out_l, late, code_l, t + PART)
        return carry

    lax.fori_loop(0, PART // 2, body, 0)
    write_codes(code_r, out_r, ROWS)
    write_codes(code_l, out_l, ROWS)


def middle_kernel(h, away, pos, tab, a, b, in_r, in_l, out_r, out_l, code_r, code_l, scale_r, scale_l):
    base_r = (pos[0] + 8 - away) % 8 * 32 + h * SUB
    base_l = (pos[0] + away) % 8 * 32 + h * SUB
    read_codes(in_r, ROWS, scale_r)
    read_codes(in_l, ROWS, scale_l)

    def body(g, carry):
        places = [g * 4 + u for u in range(4)]
        sums = [(own_sum(tab, a, b, base_r + t), own_sum(tab, a, b, base_l + t)) for t in places]
        for t, (r, l) in zip(places, sums):
            row = pl.multiple_of(t * TILE, TILE)
            encode(r + decoded(in_r, scale_r, t), out_r, row, code_r, t)
            encode(l + decoded(in_l, scale_l, t), out_l, row, code_l, t)
        return carry

    lax.fori_loop(0, SUB // 4, body, 0)
    write_codes(code_r, out_r, ROWS)
    write_codes(code_l, out_l, ROWS)


def own_kernel(pos, tab, a, b, own):
    def body(g, carry):
        sums = [own_sum(tab, a, b, pos[0] * 32 + g * 8 + u) for u in range(8)]
        for u, one in enumerate(sums):
            own[g * 8 + u] = one
        return carry

    lax.fori_loop(0, own.shape[0] // 8, body, 0)


def final_sum(own, in_r, in_l, scale_r, scale_l, h, t):
    return own[h * SUB + t] + decoded(in_r, scale_r, t) + decoded(in_l, scale_l, t)


def put_block(sums, out, code):
    for n, one in enumerate(sums):
        encode(one, out, n * TILE, code, n)
    write_codes(code, out, len(sums) * TILE)


def spread_kernel(own, in_r, in_l, unused, far, up, down, code, scale_r, scale_l):
    read_codes(in_r, ROWS, scale_r)
    read_codes(in_l, ROWS, scale_l)
    code[...] = jnp.zeros_like(code)
    total = functools.partial(final_sum, own, in_r, in_l, scale_r, scale_l, 0)
    for k in range(2):
        put_block([total(4 * k + n) for n in range(4)], far.at[k], code.at[k])
        put_block([total(8 + 2 * k + n) for n in range(2)], up.at[k], code.at[2 + k])
        put_block([total(12 + 2 * k + n) for n in range(2)], down.at[k], code.at[4 + k])


def last_kernel(own, in_r, in_l, unused, up, down, cross, home, code, scale_r, scale_l):
    read_codes(in_r, ROWS, scale_r)
    read_codes(in_l, ROWS, scale_l)
    code[...] = jnp.zeros_like(code)
    total = functools.partial(final_sum, own, in_r, in_l, scale_r, scale_l, 1)
    for k in range(2):
        put_block([total(2 * k + n) for n in range(2)], up.at[k], code.at[k])
        put_block([total(4 + 2 * k + n) for n in range(2)], down.at[k], code.at[2 + k])
    put_block([total(12 + n) for n in range(4)], cross, code.at[4])
    for n in range(4):
        home[n] = total(8 + n)


def deliver_blocks(blocks, out, tiles, scale, sem):
    started, at = [], 0
    for n, (src, row, g, first, count) in enumerate(blocks):
        read_codes(src, row + count * TILE, scale)
        for m in range(count):
            rows = src[row + m * TILE : row + (m + 1) * TILE, :].astype(jnp.int32).astype(F32)
            tiles[at + m] = rows * scale[m : m + 1, :]
        to = out.at[pl.ds((g + 8) % 8 * 4 + first, count)]
        started.append(pltpu.make_async_copy(tiles.at[pl.ds(at, count)], to, sem.at[n]))
        started[-1].start()
        at += count
    return started


WIDE, SLIM = 4 * TILE + CODE_ROWS, 2 * TILE + CODE_ROWS


def deliver_early_kernel(pos, far, up, down, swapped, home, out, tiles, scale, sem):
    col = pos[2]
    other = col + 1 - 2 * (col % 2)
    blocks = [
        (far.at[0], 0, col + 4, 0, 4),
        (up.at[0], 0, col - 2, 0, 2),
        (down.at[0], 0, col + 2, 0, 2),
        (swapped, 0, other + 4, 0, 4),
        (swapped, WIDE, other - 2, 0, 2),
        (swapped, WIDE + SLIM, other + 2, 0, 2),
    ]
    kept = pltpu.make_async_copy(home, out.at[pl.ds(col * 4, 4)], sem.at[len(blocks)])
    kept.start()
    for one in deliver_blocks(blocks, out, tiles, scale, sem) + [kept]:
        one.wait()


def deliver_late_kernel(pos, early, up, down, swapped, cross, out, tiles, scale, sem):
    col = pos[2]
    other = col + 1 - 2 * (col % 2)
    blocks = [
        (cross, 0, other, 0, 4),
        (up.at[0], 0, col - 2, 2, 2),
        (down.at[0], 0, col + 2, 2, 2),
        (swapped, 0, other - 2, 2, 2),
        (swapped, SLIM, other + 2, 2, 2),
    ]
    for one in deliver_blocks(blocks, out, tiles, scale, sem):
        one.wait()


SMEM_SPEC = pl.BlockSpec(memory_space=pltpu.SMEM)
VMEM_SPEC = pl.BlockSpec(memory_space=pltpu.VMEM)
ANY_SPEC = pl.BlockSpec(memory_space=pl.ANY)


def params(mib):
    return pltpu.CompilerParams(vmem_limit_bytes=mib * 2**20)


COST_FIRST = 2
COST_SECOND0 = 3
COST_SECOND1 = 3
COST_MIDDLE = 3
COST_OWN = 3
COST_LAST = 1


def cost(us):
    return pl.CostEstimate(flops=int(us * 1e9), bytes_accessed=int(us * 3e6), transcendentals=0)


def scratch(count):
    return [pltpu.VMEM((CODE_ROWS, TILE), F32)] * count


def message(rows):
    return jax.ShapeDtypeStruct((rows + CODE_ROWS, TILE), I16)


def step(kernel, name, weight, out_shape, scratches, after, *args):
    ins = [SMEM_SPEC, SMEM_SPEC] + [VMEM_SPEC] * (len(args) - 2) + [ANY_SPEC]
    count = len(args)

    def body(*refs):
        kernel(*refs[:count], *refs[count + 1 :])

    return pl.pallas_call(
        body,
        out_shape=out_shape,
        in_specs=ins,
        out_specs=jax.tree.map(lambda _: VMEM_SPEC, out_shape),
        scratch_shapes=scratch(scratches),
        compiler_params=params(16),
        cost_estimate=cost(weight),
        name=name,
    )(*args, after)


def own_tiles(after, *args):
    def body(pos, tab, a, b, unused, own):
        own_kernel(pos, tab, a, b, own)

    return pl.pallas_call(
        body,
        out_shape=VM((2 * SUB, TILE, TILE), F32),
        in_specs=[SMEM_SPEC] * 2 + [VMEM_SPEC] * 2 + [ANY_SPEC],
        out_specs=VMEM_SPEC,
        compiler_params=params(16),
        cost_estimate=cost(COST_OWN),
        name="own",
    )(*args, after)


def coded(tiles, *lead):
    return jax.ShapeDtypeStruct(lead + (tiles * TILE + CODE_ROWS, TILE), I16)


def finals(kernel, name, out_shape, after, *args):
    return pl.pallas_call(
        kernel,
        out_shape=out_shape,
        in_specs=[VMEM_SPEC] * 3 + [ANY_SPEC],
        out_specs=(VMEM_SPEC,) * len(out_shape),
        scratch_shapes=[pltpu.VMEM((6, CODE_ROWS, TILE), F32)] + scratch(2),
        compiler_params=params(16),
        cost_estimate=cost(COST_LAST),
        name=name,
    )(*args, after)


def deliver(kernel, name, specs, tiles, moved, aliases, *args):
    return pl.pallas_call(
        kernel,
        out_shape=jax.ShapeDtypeStruct((tiles, TILE, TILE), F32),
        in_specs=[SMEM_SPEC] + specs,
        out_specs=ANY_SPEC,
        scratch_shapes=[pltpu.VMEM((moved, TILE, TILE), F32)] + scratch(1) + [pltpu.SemaphoreType.DMA((7,))],
        input_output_aliases=aliases,
        compiler_params=params(16),
        cost_estimate=cost(COST_LAST),
        name=name,
    )(*args)


def in_hbm(x):
    return pltpu.with_memory_space_constraint(x, pltpu.HBM)


def per_device(a_tiles, a_kcol, b_tiles, b_jcol, c_jcol, c_place):
    depth, row, col = (lax.axis_size(n) for n in ("depth", "row", "col"))

    def shift(axis, size, by):
        pairs = [(i, (i + by) % size) for i in range(size)]
        return lambda x: lax.ppermute(x, axis, pairs)

    def x_split(x):
        return lax.ppermute(x, "col", [(i, (i + 2 - 4 * (i % 2)) % col) for i in range(col)])

    def y_split(x):
        pairs = []
        for r in range(row):
            for c in range(col):
                pairs.append((r * col + c, (r + 1 - 2 * (c % 2)) % row * col + c))
        return lax.ppermute(x, ("row", "col"), pairs)

    z_up, z_down = shift("depth", depth, -1), shift("depth", depth, 1)

    def swap(x):
        return lax.ppermute(x, "col", [(i, i ^ 1) for i in range(col)])

    pos = jnp.stack([lax.axis_index(n) for n in ("depth", "row", "col")]).astype(jnp.int32)
    b0 = b_tiles.reshape((-1,) + b_tiles.shape[2:])
    a0 = a_tiles.reshape((-1,) + a_tiles.shape[2:])
    q1, p1 = y_split(b0), x_split(a0)
    bp, ap = swap(b0), swap(a0)
    q2, p2 = y_split(bp), x_split(ap)
    q3, p3 = y_split(q1), x_split(p1)
    t2, s1, s2, s3 = swap(q2), swap(p1), swap(p2), swap(p3)
    tab = make_table(a_kcol, b_jcol, c_jcol, c_place)
    held = (VM((a0.shape[0], TILE, TILE), BF16), VM((b0.shape[0] + 1, TILE, TILE), BF16))
    a, b = pl.pallas_call(
        assemble_kernel,
        out_shape=held,
        in_specs=[SMEM_SPEC] + [ANY_SPEC] * 9,
        out_specs=(VMEM_SPEC, VMEM_SPEC),
        scratch_shapes=[pltpu.SemaphoreType.DMA((9,))],
        compiler_params=params(16),
        cost_estimate=cost(0),
        name="assemble",
    )(pos, in_hbm(a0), ap, p1, p2, p3, s1, in_hbm(b0), q1, t2)

    short = (message(HALF_ROWS),) * 2
    full = (message(ROWS),) * 2
    flying = []
    for h in range(2):
        if h == 0:
            r, l, a, b = pl.pallas_call(
                finish_kernel,
                out_shape=short + held,
                in_specs=[SMEM_SPEC] * 2 + [VMEM_SPEC] * 2 + [ANY_SPEC] * 3,
                out_specs=(VMEM_SPEC,) * 4,
                scratch_shapes=scratch(2) + [pltpu.SemaphoreType.DMA((3,))],
                input_output_aliases={2: 2, 3: 3},
                compiler_params=params(16),
                cost_estimate=cost(COST_FIRST),
                name="first0",
            )(pos, tab, a, b, s2, s3, q3)
        else:
            r, l = step(functools.partial(first_kernel, h), f"first{h}", COST_FIRST, short, 2, r, pos, tab, a, b)
        flying.append((z_up(r), z_down(l)))
    for hop in range(3):
        landed, flying = flying, []
        for h in range(2):
            if (hop, h) == (2, 1):
                own = r = own_tiles(r, pos, tab, a, b)
            if hop == 0:
                kernel, name = functools.partial(second_kernel, h), f"second{h}"
            else:
                kernel, name = functools.partial(middle_kernel, h, 3 - hop), f"middle{hop}{h}"
            weight = (COST_SECOND0, COST_SECOND1)[h] if hop == 0 else COST_MIDDLE
            r, l = step(kernel, name, weight, full, 4, r, pos, tab, a, b, *landed[h])
            flying.append((z_up(r), z_down(l)))
    x_up, x_down, x_far = (shift("col", col, n) for n in (2, -2, 4))
    far, up, down = finals(spread_kernel, "spread", (coded(4, 2), coded(2, 2), coded(2, 2)), r, own, *flying[0])
    far, up, down = x_far(far), x_up(up), x_down(down)
    up1, down1, cross, home = finals(
        last_kernel,
        "last",
        (coded(2, 2), coded(2, 2), coded(4), jax.ShapeDtypeStruct((4, TILE, TILE), F32)),
        up,
        own,
        *flying[1],
    )
    up1, down1, cross = x_up(up1), x_down(down1), swap(cross)
    far, down, home = lax.optimization_barrier((far, down, home))
    swapped = swap(jnp.concatenate([far[1], up[1], down[1]]))
    early = deliver(
        deliver_early_kernel, "deliver0", [VMEM_SPEC] * 5, col * 4, 16, {}, pos, far, up, down, swapped, home
    )
    swapped1 = swap(jnp.concatenate([up1[1], down1[1]]))
    return deliver(
        deliver_late_kernel,
        "deliver1",
        [ANY_SPEC] + [VMEM_SPEC] * 4,
        col * 4,
        12,
        {1: 0},
        pos,
        early,
        up1,
        down1,
        swapped1,
        cross,
    )


def solution(mesh):
    return jax.shard_map(
        per_device,
        mesh=mesh,
        in_specs=(
            P("row", "depth", "col", None),
            P("row", "depth"),
            P("depth", "col", "row", None),
            P("depth", "col"),
            P("row", "col"),
            P("row", "col"),
        ),
        out_specs=P(("depth", "row", "col"), None, None),
        check_vma=False,
    )
```

```python
import functools

import jax
import jax.numpy as jnp
from jax import lax
from jax.experimental import pallas as pl
from jax.experimental.pallas import tpu as pltpu
from jax.sharding import PartitionSpec as P

F32 = jnp.float32
I16 = jnp.int16
BF16 = jnp.bfloat16
VM = pltpu.VMEM
TOP = 32767.0
FINE = 128.0
TINY = 2.0**-110
TILE = 128
PART = 8
SUB = 16
ROWS = SUB * TILE
HALF_ROWS = PART * TILE
CODE_ROWS = 16


def select_blocks(a_kcol, b_jcol, c_jcol):
    k_rows, b_count = b_jcol.shape
    k_ids = jnp.arange(k_rows, dtype=jnp.int32)
    onehot_k = (a_kcol[:, :, None] == k_ids[None, None, :]).astype(jnp.int32)
    tile_cols = jnp.sum(onehot_k[:, :, :, None] * b_jcol[None, None, :, :], axis=2)
    matches = tile_cols[:, None, :, :] == c_jcol[:, :, None, None]
    slot_ids = jnp.arange(b_count, dtype=jnp.int32)
    chosen = jnp.sum(jnp.where(matches, slot_ids[None, None, None, :], 0), axis=3)
    located = jnp.any(matches, axis=3)
    flat_index = a_kcol[:, None, :] * b_count + chosen
    return jnp.where(located, flat_index, k_rows * b_count)


ORDER = (
    [(2, k, j) for k in range(2) for j in range(4)]
    + [(d, k, j) for d in (1, 3) for k in range(2) for j in (0, 1)]
    + [(d, k, j) for d in (1, 3) for k in range(2) for j in (2, 3)]
    + [(0, k, j) for k in range(2) for j in range(4)]
)


def make_table(a_kcol, b_jcol, c_jcol, c_place):
    col = lax.axis_index("col")
    away, core, tile = (jnp.array([entry[n] for entry in ORDER], jnp.int32) for n in range(3))
    owner = (col // 2 + away) % 4 * 2 + (col + core) % 2
    picks = select_blocks(a_kcol, b_jcol, c_jcol)
    rows, kept, slots = picks.shape
    row_ids = jnp.broadcast_to(jnp.arange(rows, dtype=jnp.int32)[:, None, None], (rows, kept, 1))
    fields = jnp.concatenate([row_ids, picks], axis=2).reshape(rows * kept, slots + 1)
    q = jnp.arange(rows * kept, dtype=jnp.int32)
    target = q // 32 * 32 + jnp.tile(owner * 4 + tile, rows * kept // 32)
    hit = c_place.reshape(1, rows * kept) == target[:, None]
    table = jnp.sum(jnp.where(hit[:, :, None], fields[None], 0), axis=1)
    return table.reshape(rows * kept * (slots + 1))


def a_place(a_out, col):
    return a_out.at[:, pl.ds(pl.multiple_of((col + 8) % 8 * 16, 16), 16), :]


def b_place(b_out, row, count):
    return b_out.at[pl.ds(0, count), pl.ds(pl.multiple_of(row % 4 * 32, 32), 32), :]


def copy_all(copies, sem):
    started = [pltpu.make_async_copy(src, dst, sem.at[n]) for n, (src, dst) in enumerate(copies)]
    for one in started:
        one.start()
    return started


def assemble_kernel(pos, a0, ap, p1, p2, p3, s1, b0, q1, t2, a_out, b_out, sem):
    row, col = pos[1], pos[2]
    core = col % 2
    other = col + 1 - 2 * core
    ahead = 4 * core - 2
    count = b0.shape[0]
    copies = [
        (a0, a_place(a_out, col)),
        (ap, a_place(a_out, other)),
        (p1, a_place(a_out, col + ahead)),
        (p2, a_place(a_out, other + ahead)),
        (p3, a_place(a_out, col + 4)),
        (s1, a_place(a_out, other - ahead)),
        (b0, b_place(b_out, row, count)),
        (q1, b_place(b_out, row + 3 + 2 * core, count)),
        (t2, b_place(b_out, row + 1 + 2 * core, count)),
    ]
    started = copy_all(copies, sem)
    b_out[count] = jnp.zeros(b_out.shape[1:], BF16)
    for one in started:
        one.wait()


def own_sum(tab, a, b, q):
    base = q * 6
    i = tab[base]
    left = jnp.concatenate([a[i * 5 + s] for s in range(5)], axis=1)
    right = jnp.concatenate([b[tab[base + 1 + s]] for s in range(5)], axis=0)
    return jnp.dot(left, right, preferred_element_type=F32)


def read_codes(ref, row, scale):
    codes = ref[pl.ds(row, CODE_ROWS), :].astype(jnp.int32).astype(F32)
    scale[...] = jnp.exp2(codes * (1.0 / FINE)) * (1.0 / TOP)


def decoded(ref, scale, t):
    rows = ref[pl.ds(pl.multiple_of(t * TILE, TILE), TILE), :]
    return rows.astype(jnp.int32).astype(F32) * scale[pl.ds(t, 1), :]


def encode(acc, out, row, codes, t):
    top = jnp.maximum(jnp.max(jnp.abs(acc), axis=0, keepdims=True), TINY)
    code = jnp.ceil(jnp.log2(top) * FINE) + 1.0
    codes[pl.ds(t, 1), :] = code
    quant = jnp.round(acc * (jnp.exp2(code * (-1.0 / FINE)) * TOP))
    out[pl.ds(row, TILE), :] = quant.astype(jnp.int32).astype(I16)


def write_codes(codes, out, row):
    out[pl.ds(row, CODE_ROWS), :] = codes[...].astype(jnp.int32).astype(I16)


def finish_kernel(pos, tab, a_in, b_in, s2, s3, q3, out_r, out_l, a, b, code_r, code_l, sem):
    row, col = pos[1], pos[2]
    core = col % 2
    copies = [
        (s2, a_place(a, col + 2 - 4 * core)),
        (s3, a_place(a, col + 5 - 2 * core)),
        (q3, b_place(b, row + 2, q3.shape[0])),
    ]
    for one in copy_all(copies, sem):
        one.wait()
    first_kernel(0, pos, tab, a, b, out_r, out_l, code_r, code_l)


def first_kernel(h, pos, tab, a, b, out_r, out_l, code_r, code_l):
    base = (pos[0] + 4) % 8 * 32 + h * SUB
    code_r[...] = jnp.zeros_like(code_r)
    code_l[...] = jnp.zeros_like(code_l)

    def body(g, carry):
        places = [g * 4 + u for u in range(4)]
        sums = [(own_sum(tab, a, b, base + t), own_sum(tab, a, b, base + PART + t)) for t in places]
        for t, (r, l) in zip(places, sums):
            row = pl.multiple_of(t * TILE, TILE)
            encode(r, out_r, row, code_r, t)
            encode(l, out_l, row, code_l, t)
        return carry

    lax.fori_loop(0, PART // 4, body, 0)
    write_codes(code_r, out_r, HALF_ROWS)
    write_codes(code_l, out_l, HALF_ROWS)


def second_kernel(h, pos, tab, a, b, in_r, in_l, out_r, out_l, code_r, code_l, scale_r, scale_l):
    base_r = (pos[0] + 5) % 8 * 32 + h * SUB
    base_l = (pos[0] + 3) % 8 * 32 + h * SUB
    read_codes(in_r, HALF_ROWS, scale_r)
    read_codes(in_l, HALF_ROWS, scale_l)

    def body(g, carry):
        places = [g * 2 + u for u in range(2)]
        sums = []
        for t in places:
            sums.append([own_sum(tab, a, b, q + t) for q in (base_r, base_r + PART, base_l, base_l + PART)])
        for t, (r, late_r, l, late_l) in zip(places, sums):
            row = pl.multiple_of(t * TILE, TILE)
            late = pl.multiple_of((t + PART) * TILE, TILE)
            encode(r + decoded(in_r, scale_r, t), out_r, row, code_r, t)
            encode(late_r, out_r, late, code_r, t + PART)
            encode(l, out_l, row, code_l, t)
            encode(late_l + decoded(in_l, scale_l, t), out_l, late, code_l, t + PART)
        return carry

    lax.fori_loop(0, PART // 2, body, 0)
    write_codes(code_r, out_r, ROWS)
    write_codes(code_l, out_l, ROWS)


def middle_kernel(h, away, pos, tab, a, b, in_r, in_l, out_r, out_l, code_r, code_l, scale_r, scale_l):
    base_r = (pos[0] + 8 - away) % 8 * 32 + h * SUB
    base_l = (pos[0] + away) % 8 * 32 + h * SUB
    read_codes(in_r, ROWS, scale_r)
    read_codes(in_l, ROWS, scale_l)

    def body(g, carry):
        places = [g * 4 + u for u in range(4)]
        sums = [(own_sum(tab, a, b, base_r + t), own_sum(tab, a, b, base_l + t)) for t in places]
        for t, (r, l) in zip(places, sums):
            row = pl.multiple_of(t * TILE, TILE)
            encode(r + decoded(in_r, scale_r, t), out_r, row, code_r, t)
            encode(l + decoded(in_l, scale_l, t), out_l, row, code_l, t)
        return carry

    lax.fori_loop(0, SUB // 4, body, 0)
    write_codes(code_r, out_r, ROWS)
    write_codes(code_l, out_l, ROWS)


def own_kernel(pos, tab, a, b, own):
    def body(g, carry):
        sums = [own_sum(tab, a, b, pos[0] * 32 + g * 8 + u) for u in range(8)]
        for u, one in enumerate(sums):
            own[g * 8 + u] = one
        return carry

    lax.fori_loop(0, own.shape[0] // 8, body, 0)


def final_sum(own, in_r, in_l, scale_r, scale_l, h, t):
    return own[h * SUB + t] + decoded(in_r, scale_r, t) + decoded(in_l, scale_l, t)


def put_block(sums, out, code):
    for n, one in enumerate(sums):
        encode(one, out, n * TILE, code, n)
    write_codes(code, out, len(sums) * TILE)


def spread_kernel(own, in_r, in_l, unused, far, up, down, code, scale_r, scale_l):
    read_codes(in_r, ROWS, scale_r)
    read_codes(in_l, ROWS, scale_l)
    code[...] = jnp.zeros_like(code)
    total = functools.partial(final_sum, own, in_r, in_l, scale_r, scale_l, 0)
    for k in range(2):
        put_block([total(4 * k + n) for n in range(4)], far.at[k], code.at[k])
        put_block([total(8 + 2 * k + n) for n in range(2)], up.at[k], code.at[2 + k])
        put_block([total(12 + 2 * k + n) for n in range(2)], down.at[k], code.at[4 + k])


def last_kernel(own, in_r, in_l, unused, up, down, cross, home, code, scale_r, scale_l):
    read_codes(in_r, ROWS, scale_r)
    read_codes(in_l, ROWS, scale_l)
    code[...] = jnp.zeros_like(code)
    total = functools.partial(final_sum, own, in_r, in_l, scale_r, scale_l, 1)
    for k in range(2):
        put_block([total(2 * k + n) for n in range(2)], up.at[k], code.at[k])
        put_block([total(4 + 2 * k + n) for n in range(2)], down.at[k], code.at[2 + k])
    put_block([total(12 + n) for n in range(4)], cross, code.at[4])
    for n in range(4):
        home[n] = total(8 + n)


def deliver_blocks(blocks, out, tiles, scale, sem):
    started, at = [], 0
    for n, (src, row, g, first, count) in enumerate(blocks):
        read_codes(src, row + count * TILE, scale)
        for m in range(count):
            rows = src[row + m * TILE : row + (m + 1) * TILE, :].astype(jnp.int32).astype(F32)
            tiles[at + m] = rows * scale[m : m + 1, :]
        to = out.at[pl.ds((g + 8) % 8 * 4 + first, count)]
        started.append(pltpu.make_async_copy(tiles.at[pl.ds(at, count)], to, sem.at[n]))
        started[-1].start()
        at += count
    return started


WIDE, SLIM = 4 * TILE + CODE_ROWS, 2 * TILE + CODE_ROWS


def deliver_first_kernel(pos, far, up, down, home, out, tiles, scale, sem):
    col = pos[2]
    blocks = [(far.at[0], 0, col + 4, 0, 4), (up.at[0], 0, col - 2, 0, 2), (down.at[0], 0, col + 2, 0, 2)]
    kept = pltpu.make_async_copy(home, out.at[pl.ds(col * 4, 4)], sem.at[len(blocks)])
    kept.start()
    for one in deliver_blocks(blocks, out, tiles, scale, sem) + [kept]:
        one.wait()


def deliver_second_kernel(pos, before, swapped, out, tiles, scale, sem):
    col = pos[2]
    other = col + 1 - 2 * (col % 2)
    blocks = [
        (swapped, 0, other + 4, 0, 4),
        (swapped, WIDE, other - 2, 0, 2),
        (swapped, WIDE + SLIM, other + 2, 0, 2),
    ]
    for one in deliver_blocks(blocks, out, tiles, scale, sem):
        one.wait()


def deliver_last_kernel(pos, before, up, down, swapped, cross, out, tiles, scale, sem):
    col = pos[2]
    other = col + 1 - 2 * (col % 2)
    blocks = [
        (up.at[0], 0, col - 2, 2, 2),
        (down.at[0], 0, col + 2, 2, 2),
        (swapped, 0, other - 2, 2, 2),
        (swapped, SLIM, other + 2, 2, 2),
        (cross, 0, other, 0, 4),
    ]
    for one in deliver_blocks(blocks, out, tiles, scale, sem):
        one.wait()


SMEM_SPEC = pl.BlockSpec(memory_space=pltpu.SMEM)
VMEM_SPEC = pl.BlockSpec(memory_space=pltpu.VMEM)
ANY_SPEC = pl.BlockSpec(memory_space=pl.ANY)


def params(mib):
    return pltpu.CompilerParams(vmem_limit_bytes=mib * 2**20)


COST_FIRST = 2
COST_SECOND0 = 3
COST_SECOND1 = 3
COST_MIDDLE = 3
COST_OWN = 3
COST_LAST = 1


def cost(us):
    return pl.CostEstimate(flops=int(us * 1e9), bytes_accessed=int(us * 3e6), transcendentals=0)


def scratch(count):
    return [pltpu.VMEM((CODE_ROWS, TILE), F32)] * count


def message(rows):
    return jax.ShapeDtypeStruct((rows + CODE_ROWS, TILE), I16)


def step(kernel, name, weight, out_shape, scratches, after, *args):
    ins = [SMEM_SPEC, SMEM_SPEC] + [VMEM_SPEC] * (len(args) - 2) + [ANY_SPEC]
    count = len(args)

    def body(*refs):
        kernel(*refs[:count], *refs[count + 1 :])

    return pl.pallas_call(
        body,
        out_shape=out_shape,
        in_specs=ins,
        out_specs=jax.tree.map(lambda _: VMEM_SPEC, out_shape),
        scratch_shapes=scratch(scratches),
        compiler_params=params(16),
        cost_estimate=cost(weight),
        name=name,
    )(*args, after)


def own_tiles(after, *args):
    def body(pos, tab, a, b, unused, own):
        own_kernel(pos, tab, a, b, own)

    return pl.pallas_call(
        body,
        out_shape=VM((2 * SUB, TILE, TILE), F32),
        in_specs=[SMEM_SPEC] * 2 + [VMEM_SPEC] * 2 + [ANY_SPEC],
        out_specs=VMEM_SPEC,
        compiler_params=params(16),
        cost_estimate=cost(COST_OWN),
        name="own",
    )(*args, after)


def coded(tiles, *lead):
    return jax.ShapeDtypeStruct(lead + (tiles * TILE + CODE_ROWS, TILE), I16)


def finals(kernel, name, out_shape, after, *args):
    return pl.pallas_call(
        kernel,
        out_shape=out_shape,
        in_specs=[VMEM_SPEC] * 3 + [ANY_SPEC],
        out_specs=(VMEM_SPEC,) * len(out_shape),
        scratch_shapes=[pltpu.VMEM((6, CODE_ROWS, TILE), F32)] + scratch(2),
        compiler_params=params(16),
        cost_estimate=cost(COST_LAST),
        name=name,
    )(*args, after)


def deliver(kernel, name, specs, tiles, moved, aliases, *args):
    return pl.pallas_call(
        kernel,
        out_shape=jax.ShapeDtypeStruct((tiles, TILE, TILE), F32),
        in_specs=[SMEM_SPEC] + specs,
        out_specs=ANY_SPEC,
        scratch_shapes=[pltpu.VMEM((moved, TILE, TILE), F32)] + scratch(1) + [pltpu.SemaphoreType.DMA((7,))],
        input_output_aliases=aliases,
        compiler_params=params(16),
        cost_estimate=cost(COST_LAST),
        name=name,
    )(*args)


def in_hbm(x):
    return pltpu.with_memory_space_constraint(x, pltpu.HBM)


def per_device(a_tiles, a_kcol, b_tiles, b_jcol, c_jcol, c_place):
    depth, row, col = (lax.axis_size(n) for n in ("depth", "row", "col"))

    def shift(axis, size, by):
        pairs = [(i, (i + by) % size) for i in range(size)]
        return lambda x: lax.ppermute(x, axis, pairs)

    def x_split(x):
        return lax.ppermute(x, "col", [(i, (i + 2 - 4 * (i % 2)) % col) for i in range(col)])

    def y_split(x):
        pairs = []
        for r in range(row):
            for c in range(col):
                pairs.append((r * col + c, (r + 1 - 2 * (c % 2)) % row * col + c))
        return lax.ppermute(x, ("row", "col"), pairs)

    z_up, z_down = shift("depth", depth, -1), shift("depth", depth, 1)

    def swap(x):
        return lax.ppermute(x, "col", [(i, i ^ 1) for i in range(col)])

    pos = jnp.stack([lax.axis_index(n) for n in ("depth", "row", "col")]).astype(jnp.int32)
    b0 = b_tiles.reshape((-1,) + b_tiles.shape[2:])
    a0 = a_tiles.reshape((-1,) + a_tiles.shape[2:])
    q1, p1 = y_split(b0), x_split(a0)
    bp, ap = swap(b0), swap(a0)
    q2, p2 = y_split(bp), x_split(ap)
    q3, p3 = y_split(q1), x_split(p1)
    t2, s1, s2, s3 = swap(q2), swap(p1), swap(p2), swap(p3)
    tab = make_table(a_kcol, b_jcol, c_jcol, c_place)
    held = (VM((a0.shape[0], TILE, TILE), BF16), VM((b0.shape[0] + 1, TILE, TILE), BF16))
    a, b = pl.pallas_call(
        assemble_kernel,
        out_shape=held,
        in_specs=[SMEM_SPEC] + [ANY_SPEC] * 9,
        out_specs=(VMEM_SPEC, VMEM_SPEC),
        scratch_shapes=[pltpu.SemaphoreType.DMA((9,))],
        compiler_params=params(16),
        cost_estimate=cost(0),
        name="assemble",
    )(pos, in_hbm(a0), ap, p1, p2, p3, s1, in_hbm(b0), q1, t2)

    short = (message(HALF_ROWS),) * 2
    full = (message(ROWS),) * 2
    flying = []
    for h in range(2):
        if h == 0:
            r, l, a, b = pl.pallas_call(
                finish_kernel,
                out_shape=short + held,
                in_specs=[SMEM_SPEC] * 2 + [VMEM_SPEC] * 2 + [ANY_SPEC] * 3,
                out_specs=(VMEM_SPEC,) * 4,
                scratch_shapes=scratch(2) + [pltpu.SemaphoreType.DMA((3,))],
                input_output_aliases={2: 2, 3: 3},
                compiler_params=params(16),
                cost_estimate=cost(COST_FIRST),
                name="first0",
            )(pos, tab, a, b, s2, s3, q3)
        else:
            r, l = step(functools.partial(first_kernel, h), f"first{h}", COST_FIRST, short, 2, r, pos, tab, a, b)
        flying.append((z_up(r), z_down(l)))
    for hop in range(3):
        landed, flying = flying, []
        for h in range(2):
            if (hop, h) == (2, 1):
                own = r = own_tiles(r, pos, tab, a, b)
            if hop == 0:
                kernel, name = functools.partial(second_kernel, h), f"second{h}"
            else:
                kernel, name = functools.partial(middle_kernel, h, 3 - hop), f"middle{hop}{h}"
            weight = (COST_SECOND0, COST_SECOND1)[h] if hop == 0 else COST_MIDDLE
            r, l = step(kernel, name, weight, full, 4, r, pos, tab, a, b, *landed[h])
            flying.append((z_up(r), z_down(l)))
    x_up, x_down, x_far = (shift("col", col, n) for n in (2, -2, 4))
    far, up, down = finals(spread_kernel, "spread", (coded(4, 2), coded(2, 2), coded(2, 2)), r, own, *flying[0])
    far, up, down = x_far(far), x_up(up), x_down(down)
    up1, down1, cross, home = finals(
        last_kernel,
        "last",
        (coded(2, 2), coded(2, 2), coded(4), jax.ShapeDtypeStruct((4, TILE, TILE), F32)),
        up,
        own,
        *flying[1],
    )
    up1, down1 = x_up(up1), x_down(down1)
    far, down, home = lax.optimization_barrier((far, down, home))
    swapped = swap(jnp.concatenate([far[1], up[1], down[1]]))
    done = deliver(deliver_first_kernel, "deliver0", [VMEM_SPEC] * 4, col * 4, 8, {}, pos, far, up, down, home)
    done, up1, down1, cross = lax.optimization_barrier((done, up1, down1, cross))
    cross = swap(cross)
    swapped1 = swap(jnp.concatenate([up1[1], down1[1]]))
    specs = [ANY_SPEC] + [VMEM_SPEC] * 4
    done = deliver(deliver_second_kernel, "deliver1", specs[:2], col * 4, 8, {1: 0}, pos, done, swapped)
    return deliver(deliver_last_kernel, "deliver2", specs, col * 4, 12, {1: 0}, pos, done, up1, down1, swapped1, cross)


def solution(mesh):
    return jax.shard_map(
        per_device,
        mesh=mesh,
        in_specs=(
            P("row", "depth", "col", None),
            P("row", "depth"),
            P("depth", "col", "row", None),
            P("depth", "col"),
            P("row", "col"),
            P("row", "col"),
        ),
        out_specs=P(("depth", "row", "col"), None, None),
        check_vma=False,
    )
```
